32 devices in a mesh: island: 4 (over z), fsdp: 8 (over y, x, core).
Axes of the slice: x: 2, y: 2, z: 4, core: 2. Of those that a mesh axis runs over, the one named last changes fastest.
Arguments:
- block_input: bfloat16 [4096, 8192], P(('island', 'fsdp')), may hold values from -170 to 170
- lang_ids: int32 [4096], P(('island', 'fsdp')), may hold values from 0 to 15
- queries: bfloat16 [4096, 4096], P(('island', 'fsdp')), may hold values from -52 to 52
- saved_keys: bfloat16 [4096, 512], P(('island', 'fsdp')), may hold values from -4 to 4
- out_grad: bfloat16 [4096, 4096], P(('island', 'fsdp')), may hold values from -70 to 70
- local_wv: bfloat16 [4, 8192, 512], P('island', 'fsdp'), may hold values from -8 to 8
- local_gain: bfloat16 [4, 16, 8192], P('island'), may hold values from -3 to 5
- outer_wv: float32 [8192, 512], P('fsdp', 'island'), may hold values from -4 to 4
- wv_momentum: float32 [8192, 512], P('fsdp', 'island'), may hold values from -1.8 to 1.8
- outer_gain: float32 [16, 8192], P('island', 'fsdp'), may hold values from 0.5 to 1.5
- gain_momentum: float32 [16, 8192], P('island', 'fsdp'), may hold values from -1.8 to 1.8
Outputs:
- new_outer_wv: float32 [8192, 512], P('fsdp', 'island')
- new_wv_momentum: float32 [8192, 512], P('fsdp', 'island')
- new_outer_gain: float32 [16, 8192], P('island', 'fsdp')
- new_gain_momentum: float32 [16, 8192], P('island', 'fsdp')
The draws below stay inside these ranges and needn't reach their ends.
All inputs are finite; a program needn't handle non-finite values.
Results may differ from the reference program's by a relative error of at most 0.00045.
Values may be sent and summed in bfloat16 or wider, within the bound.
A program may use at most 64 MiB of HBM per device.

```python
import math
import jax
import jax.numpy as jnp
from jax import lax

D = 8192
HEADS = 32
KV_HEADS = 4
HEAD_DIM = 128
LANGS = 16
SEQ_LEN = 128
TOK_DEV = 128
TOKENS = 4096
KV_WIDTH = 512
N_ISLAND = 4
N_FSDP = 8


def rough(key, shape):
    return jnp.clip(jax.random.normal(key, shape, jnp.float32), -4.0, 4.0)


def key_rows(key):
    base = rough(jax.random.fold_in(key, 31), (TOKENS, KV_HEADS * HEAD_DIM))
    return base


def draw_saved_keys(key, part):
    return key_rows(key).astype(jnp.bfloat16)


def draw_queries(key, part):
    base = rough(jax.random.fold_in(key, 32), (TOKENS, HEADS * HEAD_DIM))
    return base.astype(jnp.bfloat16)


def sequence_shared(key, width):
    shared = rough(key, (TOKENS // SEQ_LEN, width))
    return jnp.repeat(shared, SEQ_LEN, axis=0)


def draw_block_input(key, part):
    column_scale = jnp.exp(jax.random.uniform(jax.random.fold_in(key, 1), (D,), jnp.float32, 0.0, math.log(10.0)))
    column_scale = column_scale * (1.0 + 2.0 * jnp.arange(D, dtype=jnp.float32) / D)
    base = rough(jax.random.fold_in(key, 2), (TOKENS, D))
    shared = sequence_shared(jax.random.fold_in(key, 5), D)
    mixed = 0.75 * base + 0.6 * shared
    return (mixed * column_scale[None, :]).astype(jnp.bfloat16)


def draw_out_grad(key, part):
    span = TOK_DEV * N_FSDP
    ramp = 1.0 + 2.0 * (jnp.arange(TOKENS, dtype=jnp.int32) % span).astype(jnp.float32) / span
    row_scale = jnp.exp(jax.random.uniform(jax.random.fold_in(key, 3), (TOKENS,), jnp.float32, 0.0, math.log(5.0))) * ramp
    base = rough(jax.random.fold_in(key, 4), (TOKENS, HEADS * HEAD_DIM))
    shared = sequence_shared(jax.random.fold_in(key, 6), HEADS * HEAD_DIM)
    mixed = 0.75 * base + 0.4 * shared
    return (mixed * row_scale[:, None]).astype(jnp.bfloat16)


def wv_parts(key):
    shape = (D, KV_HEADS * HEAD_DIM)
    outer = rough(jax.random.fold_in(key, 41), shape)
    common = rough(jax.random.fold_in(key, 42), shape)
    own = rough(jax.random.fold_in(key, 43), (N_ISLAND,) + shape)
    ramp = 0.15 * (1.0 + 2.0 * jnp.arange(N_ISLAND, dtype=jnp.float32) / max(N_ISLAND - 1, 1))
    local = outer[None] - ramp.reshape(-1, 1, 1) * (common[None] + own)
    return (outer, local)


def draw_outer_wv(key, part):
    return wv_parts(key)[0]


def draw_local_wv(key, part):
    return wv_parts(key)[1].astype(jnp.bfloat16)


def gain_parts(key):
    shape = (LANGS, D)
    outer = 1.0 + 0.1 * rough(jax.random.fold_in(key, 51), shape)
    common = rough(jax.random.fold_in(key, 52), shape)
    own = rough(jax.random.fold_in(key, 53), (N_ISLAND,) + shape)
    ramp = 0.1 * (1.0 + 2.0 * jnp.arange(N_ISLAND, dtype=jnp.float32) / max(N_ISLAND - 1, 1))
    local = outer[None] - ramp.reshape(-1, 1, 1) * (common[None] + own)
    return (outer, local)


def draw_outer_gain(key, part):
    return gain_parts(key)[0]


def draw_local_gain(key, part):
    return gain_parts(key)[1].astype(jnp.bfloat16)


def with_ends(values, own_key, low, high):
    longest = values.shape.index(max(values.shape))
    spots = []
    for shift in (0, 1):
        where = [jax.random.randint(jax.random.fold_in(own_key, axis), (), 0, length) for axis, length in enumerate(values.shape)]
        where[longest] = (where[longest] + shift) % values.shape[longest]
        spots.append(tuple(where))
    return values.at[spots[0]].set(low).at[spots[1]].set(high)


def shard_levels(key, extent, shards, least, top_value):
    def one(axis_at, shards_of):
        draws = jax.random.uniform(jax.random.fold_in(jax.random.fold_in(key, 6), axis_at), (shards_of,), jnp.float32, least / len(shards), top_value / len(shards))
        return jnp.repeat(jnp.exp(draws), extent[axis_at] // shards_of).reshape((-1,) + (1,) * (len(extent) - axis_at - 1))

    factor_of = one(*shards[0])
    for cut in shards[1:]:
        factor_of = factor_of * one(*cut)
    return factor_of


def bell_draw(key, dims, deviation, most, pieces=(), held_as=jnp.bfloat16):
    drawn = deviation * jax.random.normal(key, dims, jnp.float32)
    if pieces:
        drawn = drawn * shard_levels(key, dims, pieces, -0.22, 0.18)
    return jnp.clip(drawn, -most, most).astype(held_as)


def setup_inputs(seed: int = 0) -> dict:
    streams_of = jax.random.split(jax.random.key(seed), 12)
    block_input = draw_block_input(jax.random.fold_in(streams_of[11], 71), 0)
    lang_ids = with_ends(jax.random.randint(streams_of[1], (TOKENS,), 0, LANGS), jax.random.fold_in(streams_of[1], 1), 0, LANGS - 1).astype(jnp.int32)
    queries = draw_queries(jax.random.fold_in(streams_of[11], 71), 0)
    saved_keys = draw_saved_keys(jax.random.fold_in(streams_of[11], 71), 0)
    out_grad = draw_out_grad(jax.random.fold_in(streams_of[11], 71), 0)
    local_wv = draw_local_wv(jax.random.fold_in(streams_of[11], 71), 0)
    local_gain = draw_local_gain(jax.random.fold_in(streams_of[11], 71), 0)
    outer_wv = draw_outer_wv(jax.random.fold_in(streams_of[11], 71), 0)
    wv_momentum = bell_draw(streams_of[8], (D, KV_WIDTH), 0.3, 1.8, ((0, 8), (1, 4)), jnp.float32)
    outer_gain = draw_outer_gain(jax.random.fold_in(streams_of[11], 71), 0)
    gain_momentum = bell_draw(streams_of[10], (LANGS, D), 0.3, 1.8, ((0, 4), (1, 8)), jnp.float32)
    return {"block_input": block_input, "lang_ids": lang_ids, "queries": queries, "saved_keys": saved_keys, "out_grad": out_grad, "local_wv": local_wv, "local_gain": local_gain, "outer_wv": outer_wv, "wv_momentum": wv_momentum, "outer_gain": outer_gain, "gain_momentum": gain_momentum}


EPSILON = 1e-05
MOMENTUM = 0.9
OUTER_RATE = 0.7
CLIP_SHARE = 0.25

def normalize(input_rows):
    widened = input_rows.astype(jnp.float32)
    average = lax.optimization_barrier(jnp.mean(widened, axis=-1, keepdims=True))
    centered = widened - average
    variance = lax.optimization_barrier(jnp.mean(centered * centered, axis=-1, keepdims=True))
    return centered * lax.rsqrt(variance + EPSILON)

def value_grad(query_seq, key_seq, grad_seq):
    length = query_seq.shape[0]
    group = HEADS // KV_HEADS
    query_f = query_seq.astype(jnp.float32).reshape(length, KV_HEADS, group, HEAD_DIM)
    key_f = key_seq.astype(jnp.float32).reshape(length, KV_HEADS, HEAD_DIM)
    scores = jnp.einsum('tkgd,skd->kgts', query_f, key_f) * HEAD_DIM ** (-0.5)
    position = jnp.arange(length, dtype=jnp.int32)
    causal = position[:, None] >= position[None, :]
    scores = jnp.where(causal, scores, -jnp.inf)
    row_top = lax.optimization_barrier(jnp.max(scores, axis=-1, keepdims=True))
    exponent = jnp.exp(scores - row_top)
    weights_bf = (exponent / lax.optimization_barrier(jnp.sum(exponent, axis=-1, keepdims=True))).astype(jnp.bfloat16)
    grad_f = grad_seq.astype(jnp.float32).reshape(length, KV_HEADS, group, HEAD_DIM)
    values = jnp.einsum('kgts,tkgd->skd', weights_bf.astype(jnp.float32), grad_f)
    return values.reshape(length, KV_HEADS * HEAD_DIM).astype(jnp.bfloat16)

def island_step(carry, item):
    input_island, lang_island, query_island, key_island, grad_island, wv_island, gain_island = item
    row_count = input_island.shape[0]
    standard = normalize(input_island)
    onehot = (lang_island[None, :] == jnp.arange(LANGS, dtype=jnp.int32)[:, None]).astype(jnp.float32)
    gain_rows = jnp.dot(onehot.T, gain_island.astype(jnp.float32), precision=lax.Precision.HIGHEST)
    normed = (standard * gain_rows).astype(jnp.bfloat16)
    sequences = row_count // SEQ_LEN
    values_grad = lax.map(lambda triple: value_grad(*triple), (query_island.reshape(sequences, SEQ_LEN, -1), key_island.reshape(sequences, SEQ_LEN, -1), grad_island.reshape(sequences, SEQ_LEN, -1)))
    values_grad = values_grad.reshape(row_count, KV_HEADS * HEAD_DIM)
    weight_scale = D ** (-0.5)
    wv_grad = jnp.dot(normed.T, values_grad, preferred_element_type=jnp.float32) * weight_scale
    input_grad = jnp.dot(values_grad, wv_island.T, preferred_element_type=jnp.float32) * weight_scale
    gain_grad = jnp.dot(onehot, standard * input_grad, precision=lax.Precision.HIGHEST)
    wv_norm = jnp.sqrt(jnp.sum(wv_grad * wv_grad))
    gain_norm = jnp.sqrt(jnp.sum(gain_grad * gain_grad))
    wv_clip = jnp.minimum(1.0, CLIP_SHARE * (D * KV_HEADS * HEAD_DIM) ** 0.5 / wv_norm)
    gain_clip = jnp.minimum(1.0, CLIP_SHARE * (LANGS * D) ** 0.5 / gain_norm)
    new_wv = wv_island.astype(jnp.float32) - wv_clip * wv_grad
    new_gain = gain_island.astype(jnp.float32) - gain_clip * gain_grad
    return ((carry[0] + new_wv, carry[1] + new_gain), None)

def reference(block_input, lang_ids, queries, saved_keys, out_grad, local_wv, local_gain, outer_wv, wv_momentum, outer_gain, gain_momentum):
    per_island = TOKENS // N_ISLAND
    items = (block_input.reshape(N_ISLAND, per_island, D), lang_ids.reshape(N_ISLAND, per_island), queries.reshape(N_ISLAND, per_island, -1), saved_keys.reshape(N_ISLAND, per_island, -1), out_grad.reshape(N_ISLAND, per_island, -1), local_wv, local_gain)
    start = (jnp.zeros((D, KV_HEADS * HEAD_DIM), jnp.float32), jnp.zeros((LANGS, D), jnp.float32))
    (sum_wv, sum_gain), _ = lax.scan(island_step, start, items)
    delta_wv = outer_wv - sum_wv / N_ISLAND
    momentum_wv = MOMENTUM * wv_momentum + delta_wv
    result_wv = outer_wv - OUTER_RATE * (delta_wv + MOMENTUM * momentum_wv)
    delta_gain = outer_gain - sum_gain / N_ISLAND
    momentum_gain = MOMENTUM * gain_momentum + delta_gain
    result_gain = outer_gain - OUTER_RATE * (delta_gain + MOMENTUM * momentum_gain)
    return (result_wv, momentum_wv, result_gain, momentum_gain)
```

```python
import jax
import jax.numpy as jnp
from jax import lax
from jax.sharding import PartitionSpec as P

HEADS = 32
KV_HEADS = 4
HEAD_DIM = 128


EPSILON = 1e-05
MOMENTUM = 0.9
OUTER_RATE = 0.7
CLIP_SHARE = 0.25


def value_grad(query_rows, key_block, grad_rows):
    length = query_rows.shape[0]
    group = HEADS // KV_HEADS
    query_four = query_rows.reshape(length, KV_HEADS, group, HEAD_DIM)
    key_three = key_block.reshape(length, KV_HEADS, HEAD_DIM)
    scores = jnp.einsum(
        "tkgd,skd->kgts", query_four, key_three, preferred_element_type=jnp.float32
    ) * HEAD_DIM ** (-0.5)
    position = jnp.arange(length, dtype=jnp.int32)
    causal = position[:, None] >= position[None, :]
    scores = jnp.where(causal, scores, -jnp.inf)
    row_top = jnp.max(scores, axis=-1, keepdims=True)
    exponent = jnp.exp(scores - row_top)
    weights_bf = (exponent / jnp.sum(exponent, axis=-1, keepdims=True)).astype(jnp.bfloat16)
    grad_four = grad_rows.reshape(length, KV_HEADS, group, HEAD_DIM)
    values = jnp.einsum("kgts,tkgd->skd", weights_bf, grad_four, preferred_element_type=jnp.float32)
    return values.reshape(length, KV_HEADS * HEAD_DIM).astype(jnp.bfloat16)


def body(
    block_input,
    lang_ids,
    queries,
    saved_keys,
    out_grad,
    local_wv,
    local_gain,
    outer_wv,
    wv_momentum,
    outer_gain,
    gain_momentum,
):
    width = block_input.shape[1]
    fsdp_count = lax.axis_size("fsdp")
    island_count = lax.axis_size("island")
    col_block = width // fsdp_count
    kv_width = local_wv.shape[2]
    lang_count = local_gain.shape[1]
    weight_scale = width ** (-0.5)
    col_begin = lax.axis_index("fsdp") * col_block
    cols = lax.all_to_all(block_input, "fsdp", split_axis=1, concat_axis=0, tiled=True)
    values_all = lax.all_gather(
        value_grad(queries, saved_keys, out_grad), "fsdp", axis=0, tiled=True
    )
    widened = block_input.astype(jnp.float32)
    average = jnp.mean(widened, axis=-1, keepdims=True)
    centered = widened - average
    variance = jnp.mean(centered * centered, axis=-1, keepdims=True)
    rows = jnp.concatenate(
        [average, lax.rsqrt(variance + EPSILON), lang_ids[:, None].astype(jnp.float32)], axis=1
    )
    rows_all = lax.all_gather(rows, "fsdp", axis=0, tiled=True)
    standard = (cols.astype(jnp.float32) - rows_all[:, 0:1]) * rows_all[:, 1:2]
    lang_table = rows_all[:, 2][None, :] == jnp.arange(lang_count, dtype=jnp.float32)[:, None]
    own_gain = lax.dynamic_slice_in_dim(local_gain[0], col_begin, col_block, 1)
    gain_rows = jnp.dot(
        lang_table.astype(jnp.bfloat16).T, own_gain, preferred_element_type=jnp.float32
    )
    normed = (standard * gain_rows).astype(jnp.bfloat16)
    weight_rows = local_wv[0]
    wv_grad = jnp.dot(normed.T, values_all, preferred_element_type=jnp.float32) * weight_scale
    input_grad = jnp.dot(values_all, weight_rows.T, preferred_element_type=jnp.float32) * weight_scale
    own_grad = jnp.dot(
        lang_table.astype(jnp.float32), standard * input_grad, precision=lax.Precision.HIGHEST
    )
    squares = lax.psum(jnp.stack([jnp.sum(wv_grad * wv_grad), jnp.sum(own_grad * own_grad)]), "fsdp")
    wv_clip = jnp.minimum(1.0, CLIP_SHARE * (width * kv_width) ** 0.5 / jnp.sqrt(squares[0]))
    gain_clip = jnp.minimum(1.0, CLIP_SHARE * (lang_count * width) ** 0.5 / jnp.sqrt(squares[1]))
    new_wv = weight_rows.astype(jnp.float32) - wv_clip * wv_grad
    new_gain = own_gain.astype(jnp.float32) - gain_clip * own_grad
    total_wv = lax.psum_scatter(new_wv, "island", scatter_dimension=1, tiled=True)
    total_gain = lax.psum_scatter(new_gain, "island", scatter_dimension=0, tiled=True)
    delta_wv = outer_wv - total_wv / island_count
    momentum_wv = MOMENTUM * wv_momentum + delta_wv
    result_wv = outer_wv - OUTER_RATE * (delta_wv + MOMENTUM * momentum_wv)
    delta_gain = outer_gain - total_gain / island_count
    momentum_gain = MOMENTUM * gain_momentum + delta_gain
    result_gain = outer_gain - OUTER_RATE * (delta_gain + MOMENTUM * momentum_gain)
    return (result_wv, momentum_wv, result_gain, momentum_gain)


def solution(mesh):
    in_specs = (
        P(("island", "fsdp"), None),
        P(("island", "fsdp")),
        P(("island", "fsdp"), None),
        P(("island", "fsdp"), None),
        P(("island", "fsdp"), None),
        P("island", "fsdp", None),
        P("island", None, None),
        P("fsdp", "island"),
        P("fsdp", "island"),
        P("island", "fsdp"),
        P("island", "fsdp"),
    )
    out_specs = (P("fsdp", "island"), P("fsdp", "island"), P("island", "fsdp"), P("island", "fsdp"))
    return jax.shard_map(body, mesh=mesh, in_specs=in_specs, out_specs=out_specs, check_vma=False)
```

```python
import functools

import jax
import jax.numpy as jnp
from jax import lax
from jax.experimental import pallas as pl
from jax.experimental.pallas import tpu as pltpu
from jax.sharding import PartitionSpec as P

HEADS = 32
KV_HEADS = 4
HEAD_DIM = 128


EPSILON = 1e-05
MOMENTUM = 0.9
OUTER_RATE = 0.7
CLIP_SHARE = 0.25


def value_grad(query_rows, key_block, grad_rows):
    length = query_rows.shape[0]
    group = HEADS // KV_HEADS
    query_four = query_rows.reshape(length, KV_HEADS, group, HEAD_DIM)
    key_three = key_block.reshape(length, KV_HEADS, HEAD_DIM)
    scores = jnp.einsum(
        "tkgd,skd->kgts", query_four, key_three, preferred_element_type=jnp.float32
    ) * HEAD_DIM ** (-0.5)
    position = jnp.arange(length, dtype=jnp.int32)
    causal = position[:, None] >= position[None, :]
    scores = jnp.where(causal, scores, -jnp.inf)
    row_top = jnp.max(scores, axis=-1, keepdims=True)
    exponent = jnp.exp(scores - row_top)
    weights_bf = (exponent / jnp.sum(exponent, axis=-1, keepdims=True)).astype(jnp.bfloat16)
    grad_four = grad_rows.reshape(length, KV_HEADS, group, HEAD_DIM)
    values = jnp.einsum("kgts,tkgd->skd", weights_bf, grad_four, preferred_element_type=jnp.float32)
    return values.reshape(length, KV_HEADS * HEAD_DIM).astype(jnp.bfloat16)


def totals_by_collectives(
    block_input,
    lang_ids,
    queries,
    saved_keys,
    out_grad,
    local_wv,
    local_gain,
):
    width = block_input.shape[1]
    fsdp_count = lax.axis_size("fsdp")
    col_block = width // fsdp_count
    kv_width = local_wv.shape[2]
    lang_count = local_gain.shape[1]
    weight_scale = width ** (-0.5)
    col_begin = lax.axis_index("fsdp") * col_block
    cols = lax.all_to_all(block_input, "fsdp", split_axis=1, concat_axis=0, tiled=True)
    values_all = lax.all_gather(
        value_grad(queries, saved_keys, out_grad), "fsdp", axis=0, tiled=True
    )
    widened = block_input.astype(jnp.float32)
    average = jnp.mean(widened, axis=-1, keepdims=True)
    centered = widened - average
    variance = jnp.mean(centered * centered, axis=-1, keepdims=True)
    rows = jnp.concatenate(
        [average, lax.rsqrt(variance + EPSILON), lang_ids[:, None].astype(jnp.float32)], axis=1
    )
    rows_all = lax.all_gather(rows, "fsdp", axis=0, tiled=True)
    standard = (cols.astype(jnp.float32) - rows_all[:, 0:1]) * rows_all[:, 1:2]
    lang_table = rows_all[:, 2][None, :] == jnp.arange(lang_count, dtype=jnp.float32)[:, None]
    own_gain = lax.dynamic_slice_in_dim(local_gain[0], col_begin, col_block, 1)
    gain_rows = jnp.dot(
        lang_table.astype(jnp.bfloat16).T, own_gain, preferred_element_type=jnp.float32
    )
    normed = (standard * gain_rows).astype(jnp.bfloat16)
    weight_rows = local_wv[0]
    wv_grad = jnp.dot(normed.T, values_all, preferred_element_type=jnp.float32) * weight_scale
    input_grad = jnp.dot(values_all, weight_rows.T, preferred_element_type=jnp.float32) * weight_scale
    own_grad = jnp.dot(
        lang_table.astype(jnp.float32), standard * input_grad, precision=lax.Precision.HIGHEST
    )
    squares = lax.psum(jnp.stack([jnp.sum(wv_grad * wv_grad), jnp.sum(own_grad * own_grad)]), "fsdp")
    wv_clip = jnp.minimum(1.0, CLIP_SHARE * (width * kv_width) ** 0.5 / jnp.sqrt(squares[0]))
    gain_clip = jnp.minimum(1.0, CLIP_SHARE * (lang_count * width) ** 0.5 / jnp.sqrt(squares[1]))
    new_wv = weight_rows.astype(jnp.float32) - wv_clip * wv_grad
    new_gain = own_gain.astype(jnp.float32) - gain_clip * own_grad
    total_wv = lax.psum_scatter(new_wv, "island", scatter_dimension=1, tiled=True)
    total_gain = lax.psum_scatter(new_gain, "island", scatter_dimension=0, tiled=True)
    return total_wv, total_gain


CHUNKS = 4
EARLY = 2


def remote(src, dst, send_sem, recv_sem, where):
    return pltpu.make_async_remote_copy(
        src_ref=src,
        dst_ref=dst,
        send_sem=send_sem,
        recv_sem=recv_sem,
        device_id=where,
        device_id_type=pl.DeviceIdType.MESH,
    )


def attend(q_v, k_v, og_v):
    length = q_v.shape[0]
    group = HEADS // KV_HEADS
    at = lax.broadcasted_iota(jnp.int32, (length, length), 0)
    key_at = lax.broadcasted_iota(jnp.int32, (length, length), 1)
    bias = jnp.where(at >= key_at, 0.0, -1e30).astype(jnp.float32)
    bias = jnp.concatenate([bias] * group, axis=0)
    parts = []
    for j in range(KV_HEADS):
        heads = [slice((j * group + g) * HEAD_DIM, (j * group + g + 1) * HEAD_DIM) for g in range(group)]
        q = jnp.concatenate([q_v[:, h] for h in heads], axis=0)
        k = k_v[:, j * HEAD_DIM : (j + 1) * HEAD_DIM]
        scores = lax.dot_general(q, k, (((1,), (1,)), ((), ())), preferred_element_type=jnp.float32)
        scores = scores * HEAD_DIM ** (-0.5) + bias
        exponent = jnp.exp(scores - jnp.max(scores, axis=1, keepdims=True))
        probs = (exponent / jnp.sum(exponent, axis=1, keepdims=True)).astype(jnp.bfloat16)
        og = jnp.concatenate([og_v[:, h] for h in heads], axis=0)
        parts.append(
            lax.dot_general(probs, og, (((0,), (0,)), ((), ())), preferred_element_type=jnp.float32)
        )
    return jnp.concatenate(parts, axis=1).astype(jnp.bfloat16)


def kernel(
    nf, ni,
    x_hbm, lang_ref, q_hbm, k_hbm, og_hbm, wv_hbm, gain_ref,
    tot_wv, tot_gain,
    x_v, q_v, k_v, og_v, wv_v, x_buf, v_buf, s_buf, mean_b, rstd_b, hot, normed,
    g_own, g_send, g_buf, lw_buf, gg_send, gg_buf, sq_buf, clip_buf,
    load_sem, own_sem, x_ss, x_rs, lw_ss, lw_rs, v_ss, v_rs, fw_ss, s_ss, s_rs,
    g_ss, g_rs, gg_ss, gg_rs, sq_ss, sq_rs, c_ss, c_rs,
):
    f = lax.axis_index("fsdp")
    i = lax.axis_index("island")
    tokens, width = x_v.shape
    kv_width = wv_v.shape[1]
    langs = gain_ref.shape[0]
    cols = width // nf
    chunk = cols // CHUNKS
    share = kv_width // ni
    gain_share = langs // ni
    scale = width ** (-0.5)
    peers = [lax.rem(f + d, nf) for d in range(1, nf)]
    zpeers = [lax.rem(i + d, ni) for d in range(1, ni)]
    core = lax.rem(f, 2)
    chip = f // 2
    sibling = chip * 2 + 1 - core
    mates = [lax.rem(chip + d, nf // 2) * 2 + core for d in range(1, nf // 2)]
    others = [lax.rem(chip + d, nf // 2) * 2 + 1 - core for d in range(1, nf // 2)]

    loads = [
        pltpu.make_async_copy(src, dst, load_sem.at[n])
        for n, (src, dst) in enumerate(
            [(q_hbm, q_v), (k_hbm, k_v), (og_hbm, og_v), (x_hbm, x_v), (wv_hbm, wv_v)]
        )
    ]
    for copy in loads:
        copy.start()

    def x_cols(owner, k):
        return pl.ds(pl.multiple_of(owner * cols + k * chunk, 128), chunk)

    own_copies = [
        pltpu.make_async_copy(x_hbm.at[:, x_cols(f, k)], x_buf.at[k, f], own_sem.at[k])
        for k in range(CHUNKS)
    ]
    for copy in own_copies:
        copy.start()

    barrier = pltpu.get_barrier_semaphore()
    for p in peers:
        pl.semaphore_signal(barrier, inc=1, device_id={"fsdp": p}, device_id_type=pl.DeviceIdType.MESH)
    for p in zpeers:
        pl.semaphore_signal(barrier, inc=1, device_id={"island": p}, device_id_type=pl.DeviceIdType.MESH)
    pl.semaphore_wait(barrier, nf - 1 + ni - 1)

    def x_copy(k, p):
        return remote(x_hbm.at[:, x_cols(p, k)], x_buf.at[k, f], x_ss.at[k, p], x_rs.at[k, f], {"fsdp": p})

    def x_wait(k, p):
        remote(x_hbm.at[:, x_cols(p, k)], x_buf.at[k, p], x_ss.at[k, p], x_rs.at[k, p], {"fsdp": p}).wait_recv()

    for k in range(EARLY):
        for p in peers:
            x_copy(k, p).start()

    def lw_copy(p, slot):
        src = wv_hbm.at[:, pl.ds(pl.multiple_of(p * share, 128), share)]
        return remote(src, lw_buf.at[slot], lw_ss.at[p], lw_rs.at[slot], {"island": p})

    for p in zpeers:
        lw_copy(p, i).start()

    for copy in loads[:3]:
        copy.wait()
    v_buf[f] = attend(q_v, k_v, og_v)

    def v_copy(slot, p, send_sem):
        return remote(v_buf.at[slot], v_buf.at[slot], send_sem, v_rs.at[slot], {"fsdp": p})

    for p in mates:
        v_copy(f, p, v_ss.at[p]).start()
    v_copy(f, sibling, v_ss.at[sibling]).start()
    for k in range(EARLY, CHUNKS):
        for p in peers:
            x_copy(k, p).start()

    loads[3].wait()
    widened = x_v[...].astype(jnp.float32)
    average = jnp.mean(widened, axis=1, keepdims=True)
    centered = x_v[...].astype(jnp.float32) - average
    rstd = lax.rsqrt(jnp.mean(centered * centered, axis=1, keepdims=True) + EPSILON)
    square = (tokens, tokens)
    eye = lax.broadcasted_iota(jnp.int32, square, 0) == lax.broadcasted_iota(jnp.int32, square, 1)

    def to_row(column):
        return jnp.sum(jnp.where(eye, jnp.broadcast_to(column, square), 0.0), axis=0, keepdims=True)

    def to_column(row):
        return jnp.sum(jnp.where(eye, jnp.broadcast_to(row, square), 0.0), axis=1, keepdims=True)

    s_buf[f] = jnp.concatenate(
        [to_row(average), to_row(rstd), lang_ref[...].astype(jnp.float32), jnp.zeros((5, tokens), jnp.float32)],
        axis=0,
    )

    def s_copy(slot, p):
        return remote(s_buf.at[slot], s_buf.at[slot], s_ss.at[p], s_rs.at[slot], {"fsdp": p})

    for p in peers:
        s_copy(f, p).start()
    for p in mates:
        v_copy(p, p, v_ss.at[p]).wait_recv()
        v_copy(p, sibling, fw_ss.at[p]).start()

    loads[4].wait()
    for copy in own_copies:
        copy.wait()
    for p in peers:
        s_copy(p, p).wait_recv()
    for s in range(nf):
        stats = s_buf[s]
        rows = pl.ds(s * tokens, tokens)
        mean_b[rows, :] = jnp.broadcast_to(to_column(stats[0:1]), square)
        rstd_b[rows, :] = jnp.broadcast_to(to_column(stats[1:2]), square)
        kinds = lax.broadcasted_iota(jnp.int32, (langs, tokens), 0).astype(jnp.float32)
        hot[:, s * tokens : (s + 1) * tokens] = jnp.where(
            jnp.broadcast_to(stats[2:3], (langs, tokens)) == kinds, 1.0, 0.0
        ).astype(jnp.bfloat16)
    v_copy(sibling, sibling, v_ss.at[sibling]).wait_recv()
    for p in others:
        v_copy(p, sibling, v_ss.at[p]).wait_recv()

    def g_copy(k, p, slot):
        rows = pl.ds(pl.multiple_of(k * chunk, 128), chunk)
        return remote(g_send.at[p, rows], g_buf.at[slot, rows], g_ss.at[k, p], g_rs.at[k, slot], {"island": p})

    def step(k, carry):
        wv_square, gain_square = carry
        for p in peers:
            x_wait(k, p)
        rows = pl.ds(pl.multiple_of(k * chunk, 128), chunk)
        weight = wv_v[rows, :]
        gain = gain_ref[:, pl.ds(pl.multiple_of(f * cols + k * chunk, 128), chunk)]
        gain_grad = jnp.zeros((langs, chunk), jnp.float32)
        for s in range(nf):
            at = slice(s * tokens, (s + 1) * tokens)
            mean = jnp.concatenate([mean_b[at, :]] * (chunk // tokens), axis=1)
            rstd = jnp.concatenate([rstd_b[at, :]] * (chunk // tokens), axis=1)
            table = hot[:, at]
            standard = (x_buf[k, s].astype(jnp.float32) - mean) * rstd
            gain_rows = lax.dot_general(table, gain, (((0,), (0,)), ((), ())), preferred_element_type=jnp.float32)
            normed[at, :] = (standard * gain_rows).astype(jnp.bfloat16)
            input_grad = (
                lax.dot_general(v_buf[s], weight, (((1,), (1,)), ((), ())), preferred_element_type=jnp.float32) * scale
            )
            product = standard * input_grad
            high = product.astype(jnp.bfloat16)
            rest = product - high.astype(jnp.float32)
            middle = rest.astype(jnp.bfloat16)
            low = (rest - middle.astype(jnp.float32)).astype(jnp.bfloat16)
            for piece in (high, middle, low):
                gain_grad = gain_grad + jnp.dot(table, piece, preferred_element_type=jnp.float32)
        values_all = v_buf[...].reshape(nf * tokens, kv_width)
        grad = (
            lax.dot_general(normed[...], values_all, (((0,), (0,)), ((), ())), preferred_element_type=jnp.float32)
            * scale
        )
        for j in range(ni):
            piece = grad[:, j * share : (j + 1) * share]
            g_own[j, rows, :] = piece
            g_send[j, rows, :] = piece.astype(jnp.bfloat16)
            own = slice(j * gain_share, (j + 1) * gain_share)
            gg_send[j, 0:gain_share, rows] = gain[own].astype(jnp.float32)
            gg_send[j, gain_share : 2 * gain_share, rows] = gain_grad[own]
        for p in zpeers:
            g_copy(k, p, i).start()
        return (
            wv_square + jnp.sum(grad * grad, axis=0, keepdims=True),
            gain_square + jnp.sum(gain_grad * gain_grad, axis=0, keepdims=True),
        )

    start = (jnp.zeros((1, kv_width), jnp.float32), jnp.zeros((1, chunk), jnp.float32))
    wv_square, gain_square = lax.fori_loop(0, CHUNKS, step, start)

    tile = (8, 128)
    first = lax.broadcasted_iota(jnp.int32, tile, 0) == 0
    sq_buf[f] = jnp.where(
        first,
        jnp.broadcast_to(jnp.sum(wv_square, axis=1, keepdims=True), tile),
        jnp.broadcast_to(jnp.sum(gain_square, axis=1, keepdims=True), tile),
    )

    def sq_copy(slot, p):
        return remote(sq_buf.at[slot], sq_buf.at[slot], sq_ss.at[p], sq_rs.at[slot], {"fsdp": p})

    def gg_copy(p, slot):
        return remote(gg_send.at[p], gg_buf.at[slot], gg_ss.at[p], gg_rs.at[slot], {"island": p})

    for p in peers:
        sq_copy(f, p).start()
    for p in zpeers:
        gg_copy(p, i).start()
    for p in peers:
        sq_copy(p, p).wait_recv()
    norm = jnp.sqrt(jnp.sum(sq_buf[...], axis=0))
    bound = jnp.where(first, CLIP_SHARE * (width * kv_width) ** 0.5, CLIP_SHARE * (langs * width) ** 0.5)
    clip_buf[i] = jnp.minimum(1.0, bound.astype(jnp.float32) / norm)

    def c_copy(slot, p):
        return remote(clip_buf.at[slot], clip_buf.at[slot], c_ss.at[p], c_rs.at[slot], {"island": p})

    for p in zpeers:
        c_copy(i, p).start()
    for p in zpeers:
        lw_copy(p, p).wait_recv()
        gg_copy(p, p).wait_recv()
        c_copy(p, p).wait_recv()
    for k in range(CHUNKS):
        for p in zpeers:
            g_copy(k, p, p).wait_recv()

    def wide(row, size):
        return jnp.concatenate([row] * (size // 128), axis=1)

    mine = clip_buf[i]
    own_gain = gg_send[i]
    total = own_gain[0:gain_share] - wide(mine[1:2], cols) * own_gain[gain_share : 2 * gain_share]
    for p in zpeers:
        theirs = gg_buf[p]
        total = total + theirs[0:gain_share] - wide(clip_buf[p][1:2], cols) * theirs[gain_share : 2 * gain_share]
    tot_gain[...] = total
    total = wv_v[:, pl.ds(pl.multiple_of(i * share, 128), share)].astype(jnp.float32) - mine[0:1] * g_own[i]
    for p in zpeers:
        total = total + lw_buf[p].astype(jnp.float32) - clip_buf[p][0:1] * g_buf[p].astype(jnp.float32)
    tot_wv[...] = total

    for p in peers:
        for k in range(CHUNKS):
            x_copy(k, p).wait_send()
        s_copy(f, p).wait_send()
        sq_copy(f, p).wait_send()
    for p in mates:
        v_copy(f, p, v_ss.at[p]).wait_send()
        v_copy(p, sibling, fw_ss.at[p]).wait_send()
    v_copy(f, sibling, v_ss.at[sibling]).wait_send()
    for p in zpeers:
        lw_copy(p, i).wait_send()
        gg_copy(p, i).wait_send()
        c_copy(i, p).wait_send()
        for k in range(CHUNKS):
            g_copy(k, p, i).wait_send()


def totals_by_kernel(block_input, lang_ids, queries, saved_keys, out_grad, local_wv, local_gain):
    nf, ni = lax.axis_size("fsdp"), lax.axis_size("island")
    tokens, width = block_input.shape
    kv_width, langs = local_wv.shape[2], local_gain.shape[1]
    cols = width // nf
    chunk, share, gain_share = cols // CHUNKS, kv_width // ni, langs // ni
    bf, f32 = jnp.bfloat16, jnp.float32
    vmem = lambda *shape, dtype=bf: pltpu.VMEM(shape, dtype)
    dma = pltpu.SemaphoreType.DMA
    hbm = pl.BlockSpec(memory_space=pl.ANY)
    held = pl.BlockSpec(memory_space=pltpu.VMEM)
    return pl.pallas_call(
        functools.partial(kernel, nf, ni),
        out_shape=(jax.ShapeDtypeStruct((cols, share), f32), jax.ShapeDtypeStruct((gain_share, cols), f32)),
        in_specs=[hbm, held, hbm, hbm, hbm, hbm, held],
        out_specs=(held, held),
        scratch_shapes=[
            vmem(tokens, width),
            vmem(*queries.shape),
            vmem(*saved_keys.shape),
            vmem(*out_grad.shape),
            vmem(cols, kv_width),
            vmem(CHUNKS, nf, tokens, chunk),
            vmem(nf, tokens, kv_width),
            vmem(nf, 8, tokens, dtype=f32),
            vmem(nf * tokens, tokens, dtype=f32),
            vmem(nf * tokens, tokens, dtype=f32),
            vmem(langs, nf * tokens),
            vmem(nf * tokens, chunk),
            vmem(ni, cols, share, dtype=f32),
            vmem(ni, cols, share),
            vmem(ni, cols, share),
            vmem(ni, cols, share),
            vmem(ni, 2 * gain_share, cols, dtype=f32),
            vmem(ni, 2 * gain_share, cols, dtype=f32),
            vmem(nf, 8, 128, dtype=f32),
            vmem(ni, 8, 128, dtype=f32),
            dma((5,)),
            dma((CHUNKS,)),
            dma((CHUNKS, nf)),
            dma((CHUNKS, nf)),
            dma((ni,)),
            dma((ni,)),
            dma((nf,)),
            dma((nf,)),
            dma((nf,)),
            dma((nf,)),
            dma((nf,)),
            dma((CHUNKS, ni)),
            dma((CHUNKS, ni)),
            dma((ni,)),
            dma((ni,)),
            dma((nf,)),
            dma((nf,)),
            dma((ni,)),
            dma((ni,)),
        ],
        compiler_params=pltpu.CompilerParams(
            collective_id=0, has_side_effects=True, vmem_limit_bytes=48 * 1024 * 1024
        ),
    )(block_input, lang_ids[None, :], queries, saved_keys, out_grad, local_wv[0], local_gain[0])


def body(
    block_input,
    lang_ids,
    queries,
    saved_keys,
    out_grad,
    local_wv,
    local_gain,
    outer_wv,
    wv_momentum,
    outer_gain,
    gain_momentum,
):
    island_count = lax.axis_size("island")
    fsdp_count = lax.axis_size("fsdp")
    whole_tiles = (
        local_wv.shape[2] % (128 * island_count) == 0
        and local_gain.shape[1] % (4 * island_count) == 0
        and block_input.shape[1] % (128 * CHUNKS * fsdp_count) == 0
        and block_input.shape[0] == 128
        and fsdp_count % 2 == 0
    )
    totals = totals_by_kernel if whole_tiles else totals_by_collectives
    total_wv, total_gain = totals(
        block_input, lang_ids, queries, saved_keys, out_grad, local_wv, local_gain
    )
    delta_wv = outer_wv - total_wv / island_count
    momentum_wv = MOMENTUM * wv_momentum + delta_wv
    result_wv = outer_wv - OUTER_RATE * (delta_wv + MOMENTUM * momentum_wv)
    delta_gain = outer_gain - total_gain / island_count
    momentum_gain = MOMENTUM * gain_momentum + delta_gain
    result_gain = outer_gain - OUTER_RATE * (delta_gain + MOMENTUM * momentum_gain)
    return (result_wv, momentum_wv, result_gain, momentum_gain)


def solution(mesh):
    in_specs = (
        P(("island", "fsdp"), None),
        P(("island", "fsdp")),
        P(("island", "fsdp"), None),
        P(("island", "fsdp"), None),
        P(("island", "fsdp"), None),
        P("island", "fsdp", None),
        P("island", None, None),
        P("fsdp", "island"),
        P("fsdp", "island"),
        P("island", "fsdp"),
        P("island", "fsdp"),
    )
    out_specs = (P("fsdp", "island"), P("fsdp", "island"), P("island", "fsdp"), P("island", "fsdp"))
    return jax.shard_map(body, mesh=mesh, in_specs=in_specs, out_specs=out_specs, check_vma=False)
```

```python
import functools

import jax
import jax.numpy as jnp
from jax import lax
from jax.experimental import pallas as pl
from jax.experimental.pallas import tpu as pltpu
from jax.sharding import PartitionSpec as P

HEADS = 32
KV_HEADS = 4
HEAD_DIM = 128


EPSILON = 1e-05
MOMENTUM = 0.9
OUTER_RATE = 0.7
CLIP_SHARE = 0.25


def value_grad(query_rows, key_block, grad_rows):
    length = query_rows.shape[0]
    group = HEADS // KV_HEADS
    query_four = query_rows.reshape(length, KV_HEADS, group, HEAD_DIM)
    key_three = key_block.reshape(length, KV_HEADS, HEAD_DIM)
    scores = jnp.einsum(
        "tkgd,skd->kgts", query_four, key_three, preferred_element_type=jnp.float32
    ) * HEAD_DIM ** (-0.5)
    position = jnp.arange(length, dtype=jnp.int32)
    causal = position[:, None] >= position[None, :]
    scores = jnp.where(causal, scores, -jnp.inf)
    row_top = jnp.max(scores, axis=-1, keepdims=True)
    exponent = jnp.exp(scores - row_top)
    weights_bf = (exponent / jnp.sum(exponent, axis=-1, keepdims=True)).astype(jnp.bfloat16)
    grad_four = grad_rows.reshape(length, KV_HEADS, group, HEAD_DIM)
    values = jnp.einsum("kgts,tkgd->skd", weights_bf, grad_four, preferred_element_type=jnp.float32)
    return values.reshape(length, KV_HEADS * HEAD_DIM).astype(jnp.bfloat16)


def totals_by_collectives(
    block_input,
    lang_ids,
    queries,
    saved_keys,
    out_grad,
    local_wv,
    local_gain,
):
    width = block_input.shape[1]
    fsdp_count = lax.axis_size("fsdp")
    col_block = width // fsdp_count
    kv_width = local_wv.shape[2]
    lang_count = local_gain.shape[1]
    weight_scale = width ** (-0.5)
    col_begin = lax.axis_index("fsdp") * col_block
    cols = lax.all_to_all(block_input, "fsdp", split_axis=1, concat_axis=0, tiled=True)
    values_all = lax.all_gather(
        value_grad(queries, saved_keys, out_grad), "fsdp", axis=0, tiled=True
    )
    widened = block_input.astype(jnp.float32)
    average = jnp.mean(widened, axis=-1, keepdims=True)
    centered = widened - average
    variance = jnp.mean(centered * centered, axis=-1, keepdims=True)
    rows = jnp.concatenate(
        [average, lax.rsqrt(variance + EPSILON), lang_ids[:, None].astype(jnp.float32)], axis=1
    )
    rows_all = lax.all_gather(rows, "fsdp", axis=0, tiled=True)
    standard = (cols.astype(jnp.float32) - rows_all[:, 0:1]) * rows_all[:, 1:2]
    lang_table = rows_all[:, 2][None, :] == jnp.arange(lang_count, dtype=jnp.float32)[:, None]
    own_gain = lax.dynamic_slice_in_dim(local_gain[0], col_begin, col_block, 1)
    gain_rows = jnp.dot(
        lang_table.astype(jnp.bfloat16).T, own_gain, preferred_element_type=jnp.float32
    )
    normed = (standard * gain_rows).astype(jnp.bfloat16)
    weight_rows = local_wv[0]
    wv_grad = jnp.dot(normed.T, values_all, preferred_element_type=jnp.float32) * weight_scale
    input_grad = jnp.dot(values_all, weight_rows.T, preferred_element_type=jnp.float32) * weight_scale
    own_grad = jnp.dot(
        lang_table.astype(jnp.float32), standard * input_grad, precision=lax.Precision.HIGHEST
    )
    squares = lax.psum(jnp.stack([jnp.sum(wv_grad * wv_grad), jnp.sum(own_grad * own_grad)]), "fsdp")
    wv_clip = jnp.minimum(1.0, CLIP_SHARE * (width * kv_width) ** 0.5 / jnp.sqrt(squares[0]))
    gain_clip = jnp.minimum(1.0, CLIP_SHARE * (lang_count * width) ** 0.5 / jnp.sqrt(squares[1]))
    new_wv = weight_rows.astype(jnp.float32) - wv_clip * wv_grad
    new_gain = own_gain.astype(jnp.float32) - gain_clip * own_grad
    total_wv = lax.psum_scatter(new_wv, "island", scatter_dimension=1, tiled=True)
    total_gain = lax.psum_scatter(new_gain, "island", scatter_dimension=0, tiled=True)
    return total_wv, total_gain


CHUNKS = 4
EARLY = 2
STEPS = 32767.0


def remote(src, dst, send_sem, recv_sem, where):
    return pltpu.make_async_remote_copy(
        src_ref=src,
        dst_ref=dst,
        send_sem=send_sem,
        recv_sem=recv_sem,
        device_id=where,
        device_id_type=pl.DeviceIdType.MESH,
    )


def to_code(scaled):
    return jnp.floor(scaled + 0.5).astype(jnp.int32).astype(jnp.int16)


def from_code(code):
    return code.astype(jnp.int32).astype(jnp.float32)


def attend(q_v, k_v, og_v):
    length = q_v.shape[0]
    group = HEADS // KV_HEADS
    at = lax.broadcasted_iota(jnp.int32, (length, length), 0)
    key_at = lax.broadcasted_iota(jnp.int32, (length, length), 1)
    bias = jnp.where(at >= key_at, 0.0, -1e30).astype(jnp.float32)
    bias = jnp.concatenate([bias] * group, axis=0)
    parts = []
    for j in range(KV_HEADS):
        heads = [slice((j * group + g) * HEAD_DIM, (j * group + g + 1) * HEAD_DIM) for g in range(group)]
        q = jnp.concatenate([q_v[:, h] for h in heads], axis=0)
        k = k_v[:, j * HEAD_DIM : (j + 1) * HEAD_DIM]
        scores = lax.dot_general(q, k, (((1,), (1,)), ((), ())), preferred_element_type=jnp.float32)
        scores = scores * HEAD_DIM ** (-0.5) + bias
        exponent = jnp.exp(scores - jnp.max(scores, axis=1, keepdims=True))
        probs = (exponent / jnp.sum(exponent, axis=1, keepdims=True)).astype(jnp.bfloat16)
        og = jnp.concatenate([og_v[:, h] for h in heads], axis=0)
        parts.append(
            lax.dot_general(probs, og, (((0,), (0,)), ((), ())), preferred_element_type=jnp.float32)
        )
    return jnp.concatenate(parts, axis=1).astype(jnp.bfloat16)


def kernel(
    nf, ni,
    x_hbm, lang_ref, q_hbm, k_hbm, og_hbm, wv_hbm, gain_ref,
    tot_wv, tot_gain,
    x_v, q_v, k_v, og_v, wv_v, x_buf, v_buf, s_buf, mean_b, rstd_b, hot, normed,
    g_own, g_send, g_buf, lw_buf, gg_send, gg_buf, sq_buf, clip_buf,
    load_sem, own_sem, x_ss, x_rs, lw_ss, lw_rs, v_ss, v_rs, fw_ss, s_ss, s_rs,
    g_ss, g_rs, gg_ss, gg_rs, sq_ss, sq_rs, c_ss, c_rs,
):
    f = lax.axis_index("fsdp")
    i = lax.axis_index("island")
    tokens, width = x_v.shape
    kv_width = wv_v.shape[1]
    langs = gain_ref.shape[0]
    cols = width // nf
    chunk = cols // CHUNKS
    share = kv_width // ni
    gain_share = langs // ni
    scale = width ** (-0.5)
    peers = [lax.rem(f + d, nf) for d in range(1, nf)]
    zpeers = [lax.rem(i + d, ni) for d in range(1, ni)]
    core = lax.rem(f, 2)
    chip = f // 2
    sibling = chip * 2 + 1 - core
    mates = [lax.rem(chip + d, nf // 2) * 2 + core for d in range(1, nf // 2)]
    others = [lax.rem(chip + d, nf // 2) * 2 + 1 - core for d in range(1, nf // 2)]

    loads = [
        pltpu.make_async_copy(src, dst, load_sem.at[n])
        for n, (src, dst) in enumerate(
            [(q_hbm, q_v), (k_hbm, k_v), (og_hbm, og_v), (x_hbm, x_v), (wv_hbm, wv_v)]
        )
    ]
    for copy in loads:
        copy.start()

    def x_cols(owner, k):
        return pl.ds(pl.multiple_of(owner * cols + k * chunk, 128), chunk)

    own_copies = [
        pltpu.make_async_copy(x_hbm.at[:, x_cols(f, k)], x_buf.at[k, f], own_sem.at[k])
        for k in range(CHUNKS)
    ]
    for copy in own_copies:
        copy.start()

    barrier = pltpu.get_barrier_semaphore()
    for p in peers:
        pl.semaphore_signal(barrier, inc=1, device_id={"fsdp": p}, device_id_type=pl.DeviceIdType.MESH)
    for p in zpeers:
        pl.semaphore_signal(barrier, inc=1, device_id={"island": p}, device_id_type=pl.DeviceIdType.MESH)
    pl.semaphore_wait(barrier, nf - 1 + ni - 1)

    def x_copy(k, p):
        return remote(x_hbm.at[:, x_cols(p, k)], x_buf.at[k, f], x_ss.at[k, p], x_rs.at[k, f], {"fsdp": p})

    def x_wait(k, p):
        remote(x_hbm.at[:, x_cols(p, k)], x_buf.at[k, p], x_ss.at[k, p], x_rs.at[k, p], {"fsdp": p}).wait_recv()

    for k in range(EARLY):
        for p in peers:
            x_copy(k, p).start()

    def lw_copy(p, slot):
        src = wv_hbm.at[:, pl.ds(pl.multiple_of(p * share, 128), share)]
        return remote(src, lw_buf.at[slot], lw_ss.at[p], lw_rs.at[slot], {"island": p})

    for p in zpeers:
        lw_copy(p, i).start()

    for copy in loads[:3]:
        copy.wait()
    v_buf[f] = attend(q_v, k_v, og_v)

    def v_copy(slot, p, send_sem):
        return remote(v_buf.at[slot], v_buf.at[slot], send_sem, v_rs.at[slot], {"fsdp": p})

    for p in mates:
        v_copy(f, p, v_ss.at[p]).start()
    v_copy(f, sibling, v_ss.at[sibling]).start()
    for p in peers:
        x_copy(EARLY, p).start()

    loads[3].wait()
    widened = x_v[...].astype(jnp.float32)
    average = jnp.mean(widened, axis=1, keepdims=True)
    centered = x_v[...].astype(jnp.float32) - average
    rstd = lax.rsqrt(jnp.mean(centered * centered, axis=1, keepdims=True) + EPSILON)
    square = (tokens, tokens)
    eye = lax.broadcasted_iota(jnp.int32, square, 0) == lax.broadcasted_iota(jnp.int32, square, 1)

    def to_row(column):
        return jnp.sum(jnp.where(eye, jnp.broadcast_to(column, square), 0.0), axis=0, keepdims=True)

    def to_column(row):
        return jnp.sum(jnp.where(eye, jnp.broadcast_to(row, square), 0.0), axis=1, keepdims=True)

    s_buf[f] = jnp.concatenate(
        [to_row(average), to_row(rstd), lang_ref[...].astype(jnp.float32), jnp.zeros((5, tokens), jnp.float32)],
        axis=0,
    )

    def s_copy(slot, p):
        return remote(s_buf.at[slot], s_buf.at[slot], s_ss.at[p], s_rs.at[slot], {"fsdp": p})

    for p in peers:
        s_copy(f, p).start()
    for p in mates:
        v_copy(p, p, v_ss.at[p]).wait_recv()
        v_copy(p, sibling, fw_ss.at[p]).start()

    loads[4].wait()
    for copy in own_copies:
        copy.wait()
    for p in peers:
        s_copy(p, p).wait_recv()
    for s in range(nf):
        stats = s_buf[s]
        rows = pl.ds(s * tokens, tokens)
        mean_b[rows, :] = jnp.broadcast_to(to_column(stats[0:1]), square)
        rstd_b[rows, :] = jnp.broadcast_to(to_column(stats[1:2]), square)
        kinds = lax.broadcasted_iota(jnp.int32, (langs, tokens), 0).astype(jnp.float32)
        hot[:, s * tokens : (s + 1) * tokens] = jnp.where(
            jnp.broadcast_to(stats[2:3], (langs, tokens)) == kinds, 1.0, 0.0
        ).astype(jnp.bfloat16)
    v_copy(sibling, sibling, v_ss.at[sibling]).wait_recv()
    for p in others:
        v_copy(p, sibling, v_ss.at[p]).wait_recv()

    def g_copy(k, p, slot):
        rows = pl.ds(pl.multiple_of(k * chunk, 128), chunk)
        return remote(g_send.at[p, rows], g_buf.at[slot, rows], g_ss.at[k, p], g_rs.at[k, slot], {"island": p})

    tile = (8, 128)
    tile_row = lax.broadcasted_iota(jnp.int32, tile, 0)

    def step(k, carry):
        wv_square, gain_square, levels = carry
        for p in peers:
            x_wait(k, p)

        @pl.when(k + EARLY + 1 < CHUNKS)
        def _():
            for p in peers:
                x_copy(k + EARLY + 1, p).start()

        rows = pl.ds(pl.multiple_of(k * chunk, 128), chunk)
        weight = wv_v[rows, :]
        gain = gain_ref[:, pl.ds(pl.multiple_of(f * cols + k * chunk, 128), chunk)]
        gain_grad = jnp.zeros((langs, chunk), jnp.float32)
        for s in range(nf):
            at = slice(s * tokens, (s + 1) * tokens)
            mean = jnp.concatenate([mean_b[at, :]] * (chunk // tokens), axis=1)
            rstd = jnp.concatenate([rstd_b[at, :]] * (chunk // tokens), axis=1)
            table = hot[:, at]
            standard = (x_buf[k, s].astype(jnp.float32) - mean) * rstd
            gain_rows = lax.dot_general(table, gain, (((0,), (0,)), ((), ())), preferred_element_type=jnp.float32)
            normed[at, :] = (standard * gain_rows).astype(jnp.bfloat16)
            input_grad = (
                lax.dot_general(v_buf[s], weight, (((1,), (1,)), ((), ())), preferred_element_type=jnp.float32) * scale
            )
            product = standard * input_grad
            high = product.astype(jnp.bfloat16)
            rest = product - high.astype(jnp.float32)
            middle = rest.astype(jnp.bfloat16)
            low = (rest - middle.astype(jnp.float32)).astype(jnp.bfloat16)
            for piece in (high, middle, low):
                gain_grad = gain_grad + jnp.dot(table, piece, preferred_element_type=jnp.float32)
        values_all = v_buf[...].reshape(nf * tokens, kv_width)
        grad = (
            lax.dot_general(normed[...], values_all, (((0,), (0,)), ((), ())), preferred_element_type=jnp.float32)
            * scale
        )
        level = jnp.max(jnp.max(jnp.abs(grad), axis=0, keepdims=True), axis=1, keepdims=True) + 1e-30
        coded = grad * (STEPS / level)
        for j in range(ni):
            piece = grad[:, j * share : (j + 1) * share]
            g_own[j, rows, :] = piece
            g_send[j, rows, :] = to_code(coded[:, j * share : (j + 1) * share])
            own = slice(j * gain_share, (j + 1) * gain_share)
            gg_send[j, 0:gain_share, rows] = gain[own].astype(jnp.float32)
            gg_send[j, gain_share : 2 * gain_share, rows] = gain_grad[own]
        for p in zpeers:
            g_copy(k, p, i).start()
        return (
            wv_square + jnp.sum(grad * grad, axis=0, keepdims=True),
            gain_square + jnp.sum(gain_grad * gain_grad, axis=0, keepdims=True),
            jnp.where(tile_row == k + 2, jnp.broadcast_to(level, tile), levels),
        )

    start = (
        jnp.zeros((1, kv_width), jnp.float32),
        jnp.zeros((1, chunk), jnp.float32),
        jnp.zeros(tile, jnp.float32),
    )
    wv_square, gain_square, levels = lax.fori_loop(0, CHUNKS, step, start)

    first = tile_row == 0
    sq_buf[f] = jnp.where(
        first,
        jnp.broadcast_to(jnp.sum(wv_square, axis=1, keepdims=True), tile),
        jnp.broadcast_to(jnp.sum(gain_square, axis=1, keepdims=True), tile),
    )

    def sq_copy(slot, p):
        return remote(sq_buf.at[slot], sq_buf.at[slot], sq_ss.at[p], sq_rs.at[slot], {"fsdp": p})

    def gg_copy(p, slot):
        return remote(gg_send.at[p], gg_buf.at[slot], gg_ss.at[p], gg_rs.at[slot], {"island": p})

    for p in peers:
        sq_copy(f, p).start()
    for p in zpeers:
        gg_copy(p, i).start()
    for p in peers:
        sq_copy(p, p).wait_recv()
    norm = jnp.sqrt(jnp.sum(sq_buf[...], axis=0))
    bound = jnp.where(first, CLIP_SHARE * (width * kv_width) ** 0.5, CLIP_SHARE * (langs * width) ** 0.5)
    clip = jnp.minimum(1.0, bound.astype(jnp.float32) / norm)
    clip_buf[i] = jnp.where(tile_row < 2, clip, clip[0:1] * levels * (1.0 / STEPS))

    def c_copy(slot, p):
        return remote(clip_buf.at[slot], clip_buf.at[slot], c_ss.at[p], c_rs.at[slot], {"island": p})

    for p in zpeers:
        c_copy(i, p).start()
    for p in zpeers:
        lw_copy(p, p).wait_recv()
        gg_copy(p, p).wait_recv()
        c_copy(p, p).wait_recv()
    for k in range(CHUNKS):
        for p in zpeers:
            g_copy(k, p, p).wait_recv()

    def wide(row, size):
        return jnp.concatenate([row] * (size // 128), axis=1)

    mine = clip_buf[i]
    own_gain = gg_send[i]
    total = own_gain[0:gain_share] - wide(mine[1:2], cols) * own_gain[gain_share : 2 * gain_share]
    for p in zpeers:
        theirs = gg_buf[p]
        total = total + theirs[0:gain_share] - wide(clip_buf[p][1:2], cols) * theirs[gain_share : 2 * gain_share]
    tot_gain[...] = total
    total = wv_v[:, pl.ds(pl.multiple_of(i * share, 128), share)].astype(jnp.float32) - mine[0:1] * g_own[i]
    for p in zpeers:
        total = total + lw_buf[p].astype(jnp.float32)
    for k in range(CHUNKS):
        rows = slice(k * chunk, (k + 1) * chunk)
        part = total[rows]
        for p in zpeers:
            part = part - clip_buf[p][k + 2 : k + 3] * from_code(g_buf[p, rows])
        tot_wv[rows, :] = part

    for p in peers:
        for k in range(CHUNKS):
            x_copy(k, p).wait_send()
        s_copy(f, p).wait_send()
        sq_copy(f, p).wait_send()
    for p in mates:
        v_copy(f, p, v_ss.at[p]).wait_send()
        v_copy(p, sibling, fw_ss.at[p]).wait_send()
    v_copy(f, sibling, v_ss.at[sibling]).wait_send()
    for p in zpeers:
        lw_copy(p, i).wait_send()
        gg_copy(p, i).wait_send()
        c_copy(i, p).wait_send()
        for k in range(CHUNKS):
            g_copy(k, p, i).wait_send()


def totals_by_kernel(block_input, lang_ids, queries, saved_keys, out_grad, local_wv, local_gain):
    nf, ni = lax.axis_size("fsdp"), lax.axis_size("island")
    tokens, width = block_input.shape
    kv_width, langs = local_wv.shape[2], local_gain.shape[1]
    cols = width // nf
    chunk, share, gain_share = cols // CHUNKS, kv_width // ni, langs // ni
    bf, f32 = jnp.bfloat16, jnp.float32
    vmem = lambda *shape, dtype=bf: pltpu.VMEM(shape, dtype)
    dma = pltpu.SemaphoreType.DMA
    hbm = pl.BlockSpec(memory_space=pl.ANY)
    held = pl.BlockSpec(memory_space=pltpu.VMEM)
    return pl.pallas_call(
        functools.partial(kernel, nf, ni),
        out_shape=(jax.ShapeDtypeStruct((cols, share), f32), jax.ShapeDtypeStruct((gain_share, cols), f32)),
        in_specs=[hbm, held, hbm, hbm, hbm, hbm, held],
        out_specs=(held, held),
        scratch_shapes=[
            vmem(tokens, width),
            vmem(*queries.shape),
            vmem(*saved_keys.shape),
            vmem(*out_grad.shape),
            vmem(cols, kv_width),
            vmem(CHUNKS, nf, tokens, chunk),
            vmem(nf, tokens, kv_width),
            vmem(nf, 8, tokens, dtype=f32),
            vmem(nf * tokens, tokens, dtype=f32),
            vmem(nf * tokens, tokens, dtype=f32),
            vmem(langs, nf * tokens),
            vmem(nf * tokens, chunk),
            vmem(ni, cols, share, dtype=f32),
            vmem(ni, cols, share, dtype=jnp.int16),
            vmem(ni, cols, share, dtype=jnp.int16),
            vmem(ni, cols, share),
            vmem(ni, 2 * gain_share, cols, dtype=f32),
            vmem(ni, 2 * gain_share, cols, dtype=f32),
            vmem(nf, 8, 128, dtype=f32),
            vmem(ni, 8, 128, dtype=f32),
            dma((5,)),
            dma((CHUNKS,)),
            dma((CHUNKS, nf)),
            dma((CHUNKS, nf)),
            dma((ni,)),
            dma((ni,)),
            dma((nf,)),
            dma((nf,)),
            dma((nf,)),
            dma((nf,)),
            dma((nf,)),
            dma((CHUNKS, ni)),
            dma((CHUNKS, ni)),
            dma((ni,)),
            dma((ni,)),
            dma((nf,)),
            dma((nf,)),
            dma((ni,)),
            dma((ni,)),
        ],
        compiler_params=pltpu.CompilerParams(
            collective_id=0, has_side_effects=True, vmem_limit_bytes=60 * 1024 * 1024
        ),
    )(block_input, lang_ids[None, :], queries, saved_keys, out_grad, local_wv[0], local_gain[0])


def body(
    block_input,
    lang_ids,
    queries,
    saved_keys,
    out_grad,
    local_wv,
    local_gain,
    outer_wv,
    wv_momentum,
    outer_gain,
    gain_momentum,
):
    island_count = lax.axis_size("island")
    fsdp_count = lax.axis_size("fsdp")
    whole_tiles = (
        local_wv.shape[2] % (128 * island_count) == 0
        and local_gain.shape[1] % (4 * island_count) == 0
        and block_input.shape[1] % (128 * CHUNKS * fsdp_count) == 0
        and block_input.shape[0] == 128
        and fsdp_count % 2 == 0
    )
    totals = totals_by_kernel if whole_tiles else totals_by_collectives
    total_wv, total_gain = totals(
        block_input, lang_ids, queries, saved_keys, out_grad, local_wv, local_gain
    )
    delta_wv = outer_wv - total_wv / island_count
    momentum_wv = MOMENTUM * wv_momentum + delta_wv
    result_wv = outer_wv - OUTER_RATE * (delta_wv + MOMENTUM * momentum_wv)
    delta_gain = outer_gain - total_gain / island_count
    momentum_gain = MOMENTUM * gain_momentum + delta_gain
    result_gain = outer_gain - OUTER_RATE * (delta_gain + MOMENTUM * momentum_gain)
    return (result_wv, momentum_wv, result_gain, momentum_gain)


def solution(mesh):
    in_specs = (
        P(("island", "fsdp"), None),
        P(("island", "fsdp")),
        P(("island", "fsdp"), None),
        P(("island", "fsdp"), None),
        P(("island", "fsdp"), None),
        P("island", "fsdp", None),
        P("island", None, None),
        P("fsdp", "island"),
        P("fsdp", "island"),
        P("island", "fsdp"),
        P("island", "fsdp"),
    )
    out_specs = (P("fsdp", "island"), P("fsdp", "island"), P("island", "fsdp"), P("island", "fsdp"))
    return jax.shard_map(body, mesh=mesh, in_specs=in_specs, out_specs=out_specs, check_vma=False)
```

```python
import functools

import jax
import jax.numpy as jnp
from jax import lax
from jax.experimental import pallas as pl
from jax.experimental.pallas import tpu as pltpu
from jax.sharding import PartitionSpec as P

HEADS = 32
KV_HEADS = 4
HEAD_DIM = 128


EPSILON = 1e-05
MOMENTUM = 0.9
OUTER_RATE = 0.7
CLIP_SHARE = 0.25


def value_grad(query_rows, key_block, grad_rows):
    length = query_rows.shape[0]
    group = HEADS // KV_HEADS
    query_four = query_rows.reshape(length, KV_HEADS, group, HEAD_DIM)
    key_three = key_block.reshape(length, KV_HEADS, HEAD_DIM)
    scores = jnp.einsum(
        "tkgd,skd->kgts", query_four, key_three, preferred_element_type=jnp.float32
    ) * HEAD_DIM ** (-0.5)
    position = jnp.arange(length, dtype=jnp.int32)
    causal = position[:, None] >= position[None, :]
    scores = jnp.where(causal, scores, -jnp.inf)
    row_top = jnp.max(scores, axis=-1, keepdims=True)
    exponent = jnp.exp(scores - row_top)
    weights_bf = (exponent / jnp.sum(exponent, axis=-1, keepdims=True)).astype(jnp.bfloat16)
    grad_four = grad_rows.reshape(length, KV_HEADS, group, HEAD_DIM)
    values = jnp.einsum("kgts,tkgd->skd", weights_bf, grad_four, preferred_element_type=jnp.float32)
    return values.reshape(length, KV_HEADS * HEAD_DIM).astype(jnp.bfloat16)


def totals_by_collectives(
    block_input,
    lang_ids,
    queries,
    saved_keys,
    out_grad,
    local_wv,
    local_gain,
):
    width = block_input.shape[1]
    fsdp_count = lax.axis_size("fsdp")
    col_block = width // fsdp_count
    kv_width = local_wv.shape[2]
    lang_count = local_gain.shape[1]
    weight_scale = width ** (-0.5)
    col_begin = lax.axis_index("fsdp") * col_block
    cols = lax.all_to_all(block_input, "fsdp", split_axis=1, concat_axis=0, tiled=True)
    values_all = lax.all_gather(
        value_grad(queries, saved_keys, out_grad), "fsdp", axis=0, tiled=True
    )
    widened = block_input.astype(jnp.float32)
    average = jnp.mean(widened, axis=-1, keepdims=True)
    centered = widened - average
    variance = jnp.mean(centered * centered, axis=-1, keepdims=True)
    rows = jnp.concatenate(
        [average, lax.rsqrt(variance + EPSILON), lang_ids[:, None].astype(jnp.float32)], axis=1
    )
    rows_all = lax.all_gather(rows, "fsdp", axis=0, tiled=True)
    standard = (cols.astype(jnp.float32) - rows_all[:, 0:1]) * rows_all[:, 1:2]
    lang_table = rows_all[:, 2][None, :] == jnp.arange(lang_count, dtype=jnp.float32)[:, None]
    own_gain = lax.dynamic_slice_in_dim(local_gain[0], col_begin, col_block, 1)
    gain_rows = jnp.dot(
        lang_table.astype(jnp.bfloat16).T, own_gain, preferred_element_type=jnp.float32
    )
    normed = (standard * gain_rows).astype(jnp.bfloat16)
    weight_rows = local_wv[0]
    wv_grad = jnp.dot(normed.T, values_all, preferred_element_type=jnp.float32) * weight_scale
    input_grad = jnp.dot(values_all, weight_rows.T, preferred_element_type=jnp.float32) * weight_scale
    own_grad = jnp.dot(
        lang_table.astype(jnp.float32), standard * input_grad, precision=lax.Precision.HIGHEST
    )
    squares = lax.psum(jnp.stack([jnp.sum(wv_grad * wv_grad), jnp.sum(own_grad * own_grad)]), "fsdp")
    wv_clip = jnp.minimum(1.0, CLIP_SHARE * (width * kv_width) ** 0.5 / jnp.sqrt(squares[0]))
    gain_clip = jnp.minimum(1.0, CLIP_SHARE * (lang_count * width) ** 0.5 / jnp.sqrt(squares[1]))
    new_wv = weight_rows.astype(jnp.float32) - wv_clip * wv_grad
    new_gain = own_gain.astype(jnp.float32) - gain_clip * own_grad
    total_wv = lax.psum_scatter(new_wv, "island", scatter_dimension=1, tiled=True)
    total_gain = lax.psum_scatter(new_gain, "island", scatter_dimension=0, tiled=True)
    return total_wv, total_gain


CHUNKS = 4
EARLY = 2
STEPS = 32767.0


def remote(src, dst, send_sem, recv_sem, where):
    return pltpu.make_async_remote_copy(
        src_ref=src,
        dst_ref=dst,
        send_sem=send_sem,
        recv_sem=recv_sem,
        device_id=where,
        device_id_type=pl.DeviceIdType.MESH,
    )


def to_code(scaled):
    return jnp.floor(scaled + 0.5).astype(jnp.int32).astype(jnp.int16)


def from_code(code):
    return code.astype(jnp.int32).astype(jnp.float32)


def attend(q_v, k_v, og_v):
    length = q_v.shape[0]
    group = HEADS // KV_HEADS
    at = lax.broadcasted_iota(jnp.int32, (length, length), 0)
    key_at = lax.broadcasted_iota(jnp.int32, (length, length), 1)
    bias = jnp.where(at >= key_at, 0.0, -1e30).astype(jnp.float32)
    bias = jnp.concatenate([bias] * group, axis=0)
    parts = []
    for j in range(KV_HEADS):
        heads = [slice((j * group + g) * HEAD_DIM, (j * group + g + 1) * HEAD_DIM) for g in range(group)]
        q = jnp.concatenate([q_v[:, h] for h in heads], axis=0)
        k = k_v[:, j * HEAD_DIM : (j + 1) * HEAD_DIM]
        scores = lax.dot_general(q, k, (((1,), (1,)), ((), ())), preferred_element_type=jnp.float32)
        scores = scores * HEAD_DIM ** (-0.5) + bias
        exponent = jnp.exp(scores - jnp.max(scores, axis=1, keepdims=True))
        probs = (exponent / jnp.sum(exponent, axis=1, keepdims=True)).astype(jnp.bfloat16)
        og = jnp.concatenate([og_v[:, h] for h in heads], axis=0)
        parts.append(
            lax.dot_general(probs, og, (((0,), (0,)), ((), ())), preferred_element_type=jnp.float32)
        )
    return jnp.concatenate(parts, axis=1).astype(jnp.bfloat16)


def kernel(
    nf, ni,
    x_hbm, lang_ref, q_hbm, k_hbm, og_hbm, wv_hbm, gain_ref,
    tot_wv, tot_gain,
    x_v, q_v, k_v, og_v, wv_v, x_buf, v_buf, s_buf, mean_b, rstd_b, hot, normed,
    g_own, g_send, g_buf, lw_buf, rl_buf, pk_send, pk_buf, levels_v, gg_send, gg_buf, sq_buf, clip_buf,
    load_sem, own_sem, x_ss, x_rs, lw_ss, lw_rs, rl_ss, rl_rs, pk_ss, pk_rs, v_ss, v_rs, fw_ss, s_ss, s_rs,
    g_ss, g_rs, gg_ss, gg_rs, sq_ss, sq_rs, c_ss, c_rs,
):
    f = lax.axis_index("fsdp")
    i = lax.axis_index("island")
    tokens, width = x_v.shape
    kv_width = wv_v.shape[1]
    langs = gain_ref.shape[0]
    cols = width // nf
    chunk = cols // CHUNKS
    share = kv_width // ni
    gain_share = langs // ni
    scale = width ** (-0.5)
    peers = [lax.rem(f + d, nf) for d in range(1, nf)]
    zpeers = [lax.rem(i + d, ni) for d in range(1, ni)]
    core = lax.rem(f, 2)
    chip = f // 2
    sibling = chip * 2 + 1 - core
    mates = [lax.rem(chip + d, nf // 2) * 2 + core for d in range(1, nf // 2)]
    others = [lax.rem(chip + d, nf // 2) * 2 + 1 - core for d in range(1, nf // 2)]

    loads = [
        pltpu.make_async_copy(src, dst, load_sem.at[n])
        for n, (src, dst) in enumerate(
            [(q_hbm, q_v), (k_hbm, k_v), (og_hbm, og_v), (x_hbm, x_v), (wv_hbm, wv_v)]
        )
    ]
    for copy in loads:
        copy.start()

    def x_cols(owner, k):
        return pl.ds(pl.multiple_of(owner * cols + k * chunk, 128), chunk)

    own_copies = [
        pltpu.make_async_copy(x_hbm.at[:, x_cols(f, k)], x_buf.at[k, f], own_sem.at[k])
        for k in range(CHUNKS)
    ]
    for copy in own_copies:
        copy.start()

    barrier = pltpu.get_barrier_semaphore()
    for p in peers:
        pl.semaphore_signal(barrier, inc=1, device_id={"fsdp": p}, device_id_type=pl.DeviceIdType.MESH)
    for p in zpeers:
        pl.semaphore_signal(barrier, inc=1, device_id={"island": p}, device_id_type=pl.DeviceIdType.MESH)
    pl.semaphore_wait(barrier, nf - 1 + ni - 1)

    def x_copy(k, p):
        return remote(x_hbm.at[:, x_cols(p, k)], x_buf.at[k, f], x_ss.at[k, p], x_rs.at[k, f], {"fsdp": p})

    def x_wait(k, p):
        remote(x_hbm.at[:, x_cols(p, k)], x_buf.at[k, p], x_ss.at[k, p], x_rs.at[k, p], {"fsdp": p}).wait_recv()

    for k in range(EARLY):
        for p in peers:
            x_copy(k, p).start()

    half = ni // 2
    side = i // half
    base, far = side * half, (1 - side) * half
    relay, far_relay = half - 1 + side, half - side
    near = [base + lax.rem(i - base + d, half) for d in range(1, half)]

    def share_of(p):
        return pl.ds(pl.multiple_of(p * share, 128), share)

    def lw_copy(p, slot):
        return remote(wv_hbm.at[:, share_of(p)], lw_buf.at[slot], lw_ss.at[p], lw_rs.at[slot], {"island": p})

    def rl_copy(e, slot, where):
        return remote(
            wv_hbm.at[:, share_of(far + e)], rl_buf.at[slot, e], rl_ss.at[e], rl_rs.at[slot, e], {"island": where}
        )

    def pk_copy(e):
        return remote(pk_send.at[e], pk_buf, pk_ss.at[e], pk_rs.at[0], {"island": far + e})

    def pack(e):
        @pl.when(i == relay)
        def _():
            total = wv_v[:, share_of(far + e)].astype(jnp.float32)
            for p in near:
                rl_copy(e, p, p).wait_recv()
                total = total + rl_buf[p, e].astype(jnp.float32)
            level = jnp.max(jnp.max(jnp.abs(total), axis=0, keepdims=True), axis=1, keepdims=True) + 1e-30
            pk_send[e] = to_code(total * (STEPS / level))
            levels_v[6 + e : 7 + e, :] = jnp.broadcast_to(level * (1.0 / STEPS), (1, 128))
            pk_copy(e).start()

    levels_v[...] = jnp.zeros_like(levels_v)

    @pl.when(i != relay)
    def _():
        for e in range(half):
            rl_copy(e, i, relay).start()

    for copy in loads[:3]:
        copy.wait()
    v_buf[f] = attend(q_v, k_v, og_v)

    def v_copy(slot, p, send_sem):
        return remote(v_buf.at[slot], v_buf.at[slot], send_sem, v_rs.at[slot], {"fsdp": p})

    for p in mates:
        v_copy(f, p, v_ss.at[p]).start()
    v_copy(f, sibling, v_ss.at[sibling]).start()
    for p in peers:
        x_copy(EARLY, p).start()
    for p in near:
        lw_copy(p, i).start()

    loads[3].wait()
    widened = x_v[...].astype(jnp.float32)
    average = jnp.mean(widened, axis=1, keepdims=True)
    centered = x_v[...].astype(jnp.float32) - average
    rstd = lax.rsqrt(jnp.mean(centered * centered, axis=1, keepdims=True) + EPSILON)
    square = (tokens, tokens)
    eye = lax.broadcasted_iota(jnp.int32, square, 0) == lax.broadcasted_iota(jnp.int32, square, 1)

    def to_row(column):
        return jnp.sum(jnp.where(eye, jnp.broadcast_to(column, square), 0.0), axis=0, keepdims=True)

    def to_column(row):
        return jnp.sum(jnp.where(eye, jnp.broadcast_to(row, square), 0.0), axis=1, keepdims=True)

    s_buf[f] = jnp.concatenate(
        [to_row(average), to_row(rstd), lang_ref[...].astype(jnp.float32), jnp.zeros((5, tokens), jnp.float32)],
        axis=0,
    )

    def s_copy(slot, p):
        return remote(s_buf.at[slot], s_buf.at[slot], s_ss.at[p], s_rs.at[slot], {"fsdp": p})

    for p in peers:
        s_copy(f, p).start()
    loads[4].wait()
    pack(0)
    for p in mates:
        v_copy(p, p, v_ss.at[p]).wait_recv()
        v_copy(p, sibling, fw_ss.at[p]).start()
    for e in range(1, half):
        pack(e)

    for copy in own_copies:
        copy.wait()
    for p in peers:
        s_copy(p, p).wait_recv()
    for s in range(nf):
        stats = s_buf[s]
        rows = pl.ds(s * tokens, tokens)
        mean_b[rows, :] = jnp.broadcast_to(to_column(stats[0:1]), square)
        rstd_b[rows, :] = jnp.broadcast_to(to_column(stats[1:2]), square)
        kinds = lax.broadcasted_iota(jnp.int32, (langs, tokens), 0).astype(jnp.float32)
        hot[:, s * tokens : (s + 1) * tokens] = jnp.where(
            jnp.broadcast_to(stats[2:3], (langs, tokens)) == kinds, 1.0, 0.0
        ).astype(jnp.bfloat16)
    v_copy(sibling, sibling, v_ss.at[sibling]).wait_recv()
    for p in others:
        v_copy(p, sibling, v_ss.at[p]).wait_recv()

    def g_copy(k, p, slot):
        rows = pl.ds(pl.multiple_of(k * chunk, 128), chunk)
        return remote(g_send.at[p, rows], g_buf.at[slot, rows], g_ss.at[k, p], g_rs.at[k, slot], {"island": p})

    tile = (8, 128)
    tile_row = lax.broadcasted_iota(jnp.int32, tile, 0)

    def step(k, carry):
        wv_square, gain_square, levels = carry
        for p in peers:
            x_wait(k, p)

        @pl.when(k + EARLY + 1 < CHUNKS)
        def _():
            for p in peers:
                x_copy(k + EARLY + 1, p).start()

        rows = pl.ds(pl.multiple_of(k * chunk, 128), chunk)
        weight = wv_v[rows, :]
        gain = gain_ref[:, pl.ds(pl.multiple_of(f * cols + k * chunk, 128), chunk)]
        gain_grad = jnp.zeros((langs, chunk), jnp.float32)
        for s in range(nf):
            at = slice(s * tokens, (s + 1) * tokens)
            mean = jnp.concatenate([mean_b[at, :]] * (chunk // tokens), axis=1)
            rstd = jnp.concatenate([rstd_b[at, :]] * (chunk // tokens), axis=1)
            table = hot[:, at]
            standard = (x_buf[k, s].astype(jnp.float32) - mean) * rstd
            gain_rows = lax.dot_general(table, gain, (((0,), (0,)), ((), ())), preferred_element_type=jnp.float32)
            normed[at, :] = (standard * gain_rows).astype(jnp.bfloat16)
            input_grad = (
                lax.dot_general(v_buf[s], weight, (((1,), (1,)), ((), ())), preferred_element_type=jnp.float32) * scale
            )
            product = standard * input_grad
            high = product.astype(jnp.bfloat16)
            rest = product - high.astype(jnp.float32)
            middle = rest.astype(jnp.bfloat16)
            low = (rest - middle.astype(jnp.float32)).astype(jnp.bfloat16)
            for piece in (high, middle, low):
                gain_grad = gain_grad + jnp.dot(table, piece, preferred_element_type=jnp.float32)
        values_all = v_buf[...].reshape(nf * tokens, kv_width)
        grad = (
            lax.dot_general(normed[...], values_all, (((0,), (0,)), ((), ())), preferred_element_type=jnp.float32)
            * scale
        )
        level = jnp.max(jnp.max(jnp.abs(grad), axis=0, keepdims=True), axis=1, keepdims=True) + 1e-30
        coded = grad * (STEPS / level)
        for j in range(ni):
            piece = grad[:, j * share : (j + 1) * share]
            g_own[j, rows, :] = piece
            g_send[j, rows, :] = to_code(coded[:, j * share : (j + 1) * share])
            own = slice(j * gain_share, (j + 1) * gain_share)
            gg_send[j, 0:gain_share, rows] = gain[own].astype(jnp.float32)
            gg_send[j, gain_share : 2 * gain_share, rows] = gain_grad[own]
        for p in zpeers:
            g_copy(k, p, i).start()
        return (
            wv_square + jnp.sum(grad * grad, axis=0, keepdims=True),
            gain_square + jnp.sum(gain_grad * gain_grad, axis=0, keepdims=True),
            jnp.where(tile_row == k + 2, jnp.broadcast_to(level, tile), levels),
        )

    start = (
        jnp.zeros((1, kv_width), jnp.float32),
        jnp.zeros((1, chunk), jnp.float32),
        jnp.zeros(tile, jnp.float32),
    )
    wv_square, gain_square, levels = lax.fori_loop(0, CHUNKS, step, start)

    first = tile_row == 0
    sq_buf[f] = jnp.where(
        first,
        jnp.broadcast_to(jnp.sum(wv_square, axis=1, keepdims=True), tile),
        jnp.broadcast_to(jnp.sum(gain_square, axis=1, keepdims=True), tile),
    )

    def sq_copy(slot, p):
        return remote(sq_buf.at[slot], sq_buf.at[slot], sq_ss.at[p], sq_rs.at[slot], {"fsdp": p})

    def gg_copy(p, slot):
        return remote(gg_send.at[p], gg_buf.at[slot], gg_ss.at[p], gg_rs.at[slot], {"island": p})

    for p in peers:
        sq_copy(f, p).start()
    for p in zpeers:
        gg_copy(p, i).start()
    for p in peers:
        sq_copy(p, p).wait_recv()
    norm = jnp.sqrt(jnp.sum(sq_buf[...], axis=0))
    bound = jnp.where(first, CLIP_SHARE * (width * kv_width) ** 0.5, CLIP_SHARE * (langs * width) ** 0.5)
    clip = jnp.minimum(1.0, bound.astype(jnp.float32) / norm)
    coded_clip = clip[0:1] * levels * (1.0 / STEPS)
    clip_buf[i] = jnp.where(tile_row < 2, clip, jnp.where(tile_row < CHUNKS + 2, coded_clip, levels_v[...]))

    def c_copy(slot, p):
        return remote(clip_buf.at[slot], clip_buf.at[slot], c_ss.at[p], c_rs.at[slot], {"island": p})

    for p in zpeers:
        c_copy(i, p).start()
    for p in near:
        lw_copy(p, p).wait_recv()
    for p in zpeers:
        gg_copy(p, p).wait_recv()
        c_copy(p, p).wait_recv()
    remote(pk_send.at[0], pk_buf, pk_ss.at[0], pk_rs.at[0], {"island": far_relay}).wait_recv()

    def wide(row, size):
        return jnp.concatenate([row] * (size // 128), axis=1)

    mine = clip_buf[i]
    own_gain = gg_send[i]
    total = own_gain[0:gain_share] - wide(mine[1:2], cols) * own_gain[gain_share : 2 * gain_share]
    for p in zpeers:
        theirs = gg_buf[p]
        total = total + theirs[0:gain_share] - wide(clip_buf[p][1:2], cols) * theirs[gain_share : 2 * gain_share]
    tot_gain[...] = total
    total = wv_v[:, pl.ds(pl.multiple_of(i * share, 128), share)].astype(jnp.float32) - mine[0:1] * g_own[i]
    for p in near:
        total = total + lw_buf[p].astype(jnp.float32)
    far_levels = clip_buf[far_relay]
    total = total + jnp.where(i == base, far_levels[6:7], far_levels[7:8]) * from_code(pk_buf[...])
    for k in range(CHUNKS):
        rows = slice(k * chunk, (k + 1) * chunk)
        part = total[rows]
        for p in zpeers:
            g_copy(k, p, p).wait_recv()
            part = part - clip_buf[p][k + 2 : k + 3] * from_code(g_buf[p, rows])
        tot_wv[rows, :] = part

    for p in peers:
        for k in range(CHUNKS):
            x_copy(k, p).wait_send()
        s_copy(f, p).wait_send()
        sq_copy(f, p).wait_send()
    for p in mates:
        v_copy(f, p, v_ss.at[p]).wait_send()
        v_copy(p, sibling, fw_ss.at[p]).wait_send()
    v_copy(f, sibling, v_ss.at[sibling]).wait_send()
    for p in near:
        lw_copy(p, i).wait_send()

    @pl.when(i != relay)
    def _():
        for e in range(half):
            rl_copy(e, i, relay).wait_send()

    @pl.when(i == relay)
    def _():
        for e in range(half):
            pk_copy(e).wait_send()

    for p in zpeers:
        gg_copy(p, i).wait_send()
        c_copy(i, p).wait_send()
        for k in range(CHUNKS):
            g_copy(k, p, i).wait_send()


def totals_by_kernel(block_input, lang_ids, queries, saved_keys, out_grad, local_wv, local_gain):
    nf, ni = lax.axis_size("fsdp"), lax.axis_size("island")
    tokens, width = block_input.shape
    kv_width, langs = local_wv.shape[2], local_gain.shape[1]
    cols = width // nf
    chunk, share, gain_share = cols // CHUNKS, kv_width // ni, langs // ni
    bf, f32 = jnp.bfloat16, jnp.float32
    vmem = lambda *shape, dtype=bf: pltpu.VMEM(shape, dtype)
    dma = pltpu.SemaphoreType.DMA
    hbm = pl.BlockSpec(memory_space=pl.ANY)
    held = pl.BlockSpec(memory_space=pltpu.VMEM)
    return pl.pallas_call(
        functools.partial(kernel, nf, ni),
        out_shape=(jax.ShapeDtypeStruct((cols, share), f32), jax.ShapeDtypeStruct((gain_share, cols), f32)),
        in_specs=[hbm, held, hbm, hbm, hbm, hbm, held],
        out_specs=(held, held),
        scratch_shapes=[
            vmem(tokens, width),
            vmem(*queries.shape),
            vmem(*saved_keys.shape),
            vmem(*out_grad.shape),
            vmem(cols, kv_width),
            vmem(CHUNKS, nf, tokens, chunk),
            vmem(nf, tokens, kv_width),
            vmem(nf, 8, tokens, dtype=f32),
            vmem(nf * tokens, tokens, dtype=f32),
            vmem(nf * tokens, tokens, dtype=f32),
            vmem(langs, nf * tokens),
            vmem(nf * tokens, chunk),
            vmem(ni, cols, share, dtype=f32),
            vmem(ni, cols, share, dtype=jnp.int16),
            vmem(ni, cols, share, dtype=jnp.int16),
            vmem(ni, cols, share),
            vmem(ni, ni // 2, cols, share),
            vmem(ni // 2, cols, share, dtype=jnp.int16),
            vmem(cols, share, dtype=jnp.int16),
            vmem(8, 128, dtype=f32),
            vmem(ni, 2 * gain_share, cols, dtype=f32),
            vmem(ni, 2 * gain_share, cols, dtype=f32),
            vmem(nf, 8, 128, dtype=f32),
            vmem(ni, 8, 128, dtype=f32),
            dma((5,)),
            dma((CHUNKS,)),
            dma((CHUNKS, nf)),
            dma((CHUNKS, nf)),
            dma((ni,)),
            dma((ni,)),
            dma((ni // 2,)),
            dma((ni, ni // 2)),
            dma((ni // 2,)),
            dma((1,)),
            dma((nf,)),
            dma((nf,)),
            dma((nf,)),
            dma((nf,)),
            dma((nf,)),
            dma((CHUNKS, ni)),
            dma((CHUNKS, ni)),
            dma((ni,)),
            dma((ni,)),
            dma((nf,)),
            dma((nf,)),
            dma((ni,)),
            dma((ni,)),
        ],
        compiler_params=pltpu.CompilerParams(
            collective_id=0, has_side_effects=True, vmem_limit_bytes=60 * 1024 * 1024
        ),
    )(block_input, lang_ids[None, :], queries, saved_keys, out_grad, local_wv[0], local_gain[0])


def body(
    block_input,
    lang_ids,
    queries,
    saved_keys,
    out_grad,
    local_wv,
    local_gain,
    outer_wv,
    wv_momentum,
    outer_gain,
    gain_momentum,
):
    island_count = lax.axis_size("island")
    fsdp_count = lax.axis_size("fsdp")
    whole_tiles = (
        local_wv.shape[2] % (128 * island_count) == 0
        and local_gain.shape[1] % (4 * island_count) == 0
        and block_input.shape[1] % (128 * CHUNKS * fsdp_count) == 0
        and block_input.shape[0] == 128
        and fsdp_count % 2 == 0
        and island_count in (2, 4)
    )
    totals = totals_by_kernel if whole_tiles else totals_by_collectives
    total_wv, total_gain = totals(
        block_input, lang_ids, queries, saved_keys, out_grad, local_wv, local_gain
    )
    delta_wv = outer_wv - total_wv / island_count
    momentum_wv = MOMENTUM * wv_momentum + delta_wv
    result_wv = outer_wv - OUTER_RATE * (delta_wv + MOMENTUM * momentum_wv)
    delta_gain = outer_gain - total_gain / island_count
    momentum_gain = MOMENTUM * gain_momentum + delta_gain
    result_gain = outer_gain - OUTER_RATE * (delta_gain + MOMENTUM * momentum_gain)
    return (result_wv, momentum_wv, result_gain, momentum_gain)


def solution(mesh):
    in_specs = (
        P(("island", "fsdp"), None),
        P(("island", "fsdp")),
        P(("island", "fsdp"), None),
        P(("island", "fsdp"), None),
        P(("island", "fsdp"), None),
        P("island", "fsdp", None),
        P("island", None, None),
        P("fsdp", "island"),
        P("fsdp", "island"),
        P("island", "fsdp"),
        P("island", "fsdp"),
    )
    out_specs = (P("fsdp", "island"), P("fsdp", "island"), P("island", "fsdp"), P("island", "fsdp"))
    return jax.shard_map(body, mesh=mesh, in_specs=in_specs, out_specs=out_specs, check_vma=False)
```

```python
import functools

import jax
import jax.numpy as jnp
from jax import lax
from jax.experimental import pallas as pl
from jax.experimental.pallas import tpu as pltpu
from jax.sharding import PartitionSpec as P

HEADS = 32
KV_HEADS = 4
HEAD_DIM = 128


EPSILON = 1e-05
MOMENTUM = 0.9
OUTER_RATE = 0.7
CLIP_SHARE = 0.25


def value_grad(query_rows, key_block, grad_rows):
    length = query_rows.shape[0]
    group = HEADS // KV_HEADS
    query_four = query_rows.reshape(length, KV_HEADS, group, HEAD_DIM)
    key_three = key_block.reshape(length, KV_HEADS, HEAD_DIM)
    scores = jnp.einsum(
        "tkgd,skd->kgts", query_four, key_three, preferred_element_type=jnp.float32
    ) * HEAD_DIM ** (-0.5)
    position = jnp.arange(length, dtype=jnp.int32)
    causal = position[:, None] >= position[None, :]
    scores = jnp.where(causal, scores, -jnp.inf)
    row_top = jnp.max(scores, axis=-1, keepdims=True)
    exponent = jnp.exp(scores - row_top)
    weights_bf = (exponent / jnp.sum(exponent, axis=-1, keepdims=True)).astype(jnp.bfloat16)
    grad_four = grad_rows.reshape(length, KV_HEADS, group, HEAD_DIM)
    values = jnp.einsum("kgts,tkgd->skd", weights_bf, grad_four, preferred_element_type=jnp.float32)
    return values.reshape(length, KV_HEADS * HEAD_DIM).astype(jnp.bfloat16)


def totals_by_collectives(
    block_input,
    lang_ids,
    queries,
    saved_keys,
    out_grad,
    local_wv,
    local_gain,
):
    width = block_input.shape[1]
    fsdp_count = lax.axis_size("fsdp")
    col_block = width // fsdp_count
    kv_width = local_wv.shape[2]
    lang_count = local_gain.shape[1]
    weight_scale = width ** (-0.5)
    col_begin = lax.axis_index("fsdp") * col_block
    cols = lax.all_to_all(block_input, "fsdp", split_axis=1, concat_axis=0, tiled=True)
    values_all = lax.all_gather(
        value_grad(queries, saved_keys, out_grad), "fsdp", axis=0, tiled=True
    )
    widened = block_input.astype(jnp.float32)
    average = jnp.mean(widened, axis=-1, keepdims=True)
    centered = widened - average
    variance = jnp.mean(centered * centered, axis=-1, keepdims=True)
    rows = jnp.concatenate(
        [average, lax.rsqrt(variance + EPSILON), lang_ids[:, None].astype(jnp.float32)], axis=1
    )
    rows_all = lax.all_gather(rows, "fsdp", axis=0, tiled=True)
    standard = (cols.astype(jnp.float32) - rows_all[:, 0:1]) * rows_all[:, 1:2]
    lang_table = rows_all[:, 2][None, :] == jnp.arange(lang_count, dtype=jnp.float32)[:, None]
    own_gain = lax.dynamic_slice_in_dim(local_gain[0], col_begin, col_block, 1)
    gain_rows = jnp.dot(
        lang_table.astype(jnp.bfloat16).T, own_gain, preferred_element_type=jnp.float32
    )
    normed = (standard * gain_rows).astype(jnp.bfloat16)
    weight_rows = local_wv[0]
    wv_grad = jnp.dot(normed.T, values_all, preferred_element_type=jnp.float32) * weight_scale
    input_grad = jnp.dot(values_all, weight_rows.T, preferred_element_type=jnp.float32) * weight_scale
    own_grad = jnp.dot(
        lang_table.astype(jnp.float32), standard * input_grad, precision=lax.Precision.HIGHEST
    )
    squares = lax.psum(jnp.stack([jnp.sum(wv_grad * wv_grad), jnp.sum(own_grad * own_grad)]), "fsdp")
    wv_clip = jnp.minimum(1.0, CLIP_SHARE * (width * kv_width) ** 0.5 / jnp.sqrt(squares[0]))
    gain_clip = jnp.minimum(1.0, CLIP_SHARE * (lang_count * width) ** 0.5 / jnp.sqrt(squares[1]))
    new_wv = weight_rows.astype(jnp.float32) - wv_clip * wv_grad
    new_gain = own_gain.astype(jnp.float32) - gain_clip * own_grad
    total_wv = lax.psum_scatter(new_wv, "island", scatter_dimension=1, tiled=True)
    total_gain = lax.psum_scatter(new_gain, "island", scatter_dimension=0, tiled=True)
    return total_wv, total_gain


CHUNKS = 4
EARLY = 2
STEPS = 32767.0


def remote(src, dst, send_sem, recv_sem, where):
    return pltpu.make_async_remote_copy(
        src_ref=src,
        dst_ref=dst,
        send_sem=send_sem,
        recv_sem=recv_sem,
        device_id=where,
        device_id_type=pl.DeviceIdType.MESH,
    )


def to_code(scaled):
    return jnp.floor(scaled + 0.5).astype(jnp.int32).astype(jnp.int16)


def from_code(code):
    return code.astype(jnp.int32).astype(jnp.float32)


def attend(q_v, k_v, og_v):
    length = q_v.shape[0]
    group = HEADS // KV_HEADS
    at = lax.broadcasted_iota(jnp.int32, (length, length), 0)
    key_at = lax.broadcasted_iota(jnp.int32, (length, length), 1)
    bias = jnp.where(at >= key_at, 0.0, -1e30).astype(jnp.float32)
    bias = jnp.concatenate([bias] * group, axis=0)
    parts = []
    for j in range(KV_HEADS):
        heads = [slice((j * group + g) * HEAD_DIM, (j * group + g + 1) * HEAD_DIM) for g in range(group)]
        q = jnp.concatenate([q_v[:, h] for h in heads], axis=0)
        k = k_v[:, j * HEAD_DIM : (j + 1) * HEAD_DIM]
        scores = lax.dot_general(q, k, (((1,), (1,)), ((), ())), preferred_element_type=jnp.float32)
        scores = scores * HEAD_DIM ** (-0.5) + bias
        exponent = jnp.exp(scores - jnp.max(scores, axis=1, keepdims=True))
        probs = (exponent / jnp.sum(exponent, axis=1, keepdims=True)).astype(jnp.bfloat16)
        og = jnp.concatenate([og_v[:, h] for h in heads], axis=0)
        parts.append(
            lax.dot_general(probs, og, (((0,), (0,)), ((), ())), preferred_element_type=jnp.float32)
        )
    return jnp.concatenate(parts, axis=1).astype(jnp.bfloat16)


def kernel(
    nf, ni,
    x_hbm, lang_ref, q_hbm, k_hbm, og_hbm, wv_hbm, gain_ref,
    tot_wv, tot_gain,
    x_v, q_v, k_v, og_v, wv_v, x_buf, v_buf, s_buf, mean_b, rstd_b, hot, normed, wide_b, split_b,
    g_own, g_send, g_buf, lw_buf, rl_buf, pk_send, pk_buf, levels_v, gg_send, gg_buf, sq_buf, clip_buf,
    load_sem, own_sem, x_ss, x_rs, lw_ss, lw_rs, rl_ss, rl_rs, pk_ss, pk_rs, v_ss, v_rs, fw_ss, s_ss, s_rs,
    g_ss, g_rs, gg_ss, gg_rs, sq_ss, sq_rs, c_ss, c_rs,
):
    f = lax.axis_index("fsdp")
    i = lax.axis_index("island")
    tokens, width = x_v.shape
    kv_width = wv_v.shape[1]
    langs = gain_ref.shape[0]
    cols = width // nf
    chunk = cols // CHUNKS
    share = kv_width // ni
    gain_share = langs // ni
    scale = width ** (-0.5)
    peers = [lax.rem(f + d, nf) for d in range(1, nf)]
    zpeers = [lax.rem(i + d, ni) for d in range(1, ni)]
    core = lax.rem(f, 2)
    chip = f // 2
    sibling = chip * 2 + 1 - core
    mates = [lax.rem(chip + d, nf // 2) * 2 + core for d in range(1, nf // 2)]
    others = [lax.rem(chip + d, nf // 2) * 2 + 1 - core for d in range(1, nf // 2)]

    loads = [
        pltpu.make_async_copy(src, dst, load_sem.at[n])
        for n, (src, dst) in enumerate(
            [(q_hbm, q_v), (k_hbm, k_v), (og_hbm, og_v), (x_hbm, x_v), (wv_hbm, wv_v)]
        )
    ]
    for copy in loads:
        copy.start()

    def x_cols(owner, k):
        return pl.ds(pl.multiple_of(owner * cols + k * chunk, 128), chunk)

    own_copies = [
        pltpu.make_async_copy(x_hbm.at[:, x_cols(f, k)], x_buf.at[k, f], own_sem.at[k])
        for k in range(CHUNKS)
    ]
    for copy in own_copies:
        copy.start()

    barrier = pltpu.get_barrier_semaphore()
    for p in peers:
        pl.semaphore_signal(barrier, inc=1, device_id={"fsdp": p}, device_id_type=pl.DeviceIdType.MESH)
    for p in zpeers:
        pl.semaphore_signal(barrier, inc=1, device_id={"island": p}, device_id_type=pl.DeviceIdType.MESH)
    pl.semaphore_wait(barrier, nf - 1 + ni - 1)

    def x_copy(k, p):
        return remote(x_hbm.at[:, x_cols(p, k)], x_buf.at[k, f], x_ss.at[k, p], x_rs.at[k, f], {"fsdp": p})

    def x_wait(k, p):
        remote(x_hbm.at[:, x_cols(p, k)], x_buf.at[k, p], x_ss.at[k, p], x_rs.at[k, p], {"fsdp": p}).wait_recv()

    for k in range(EARLY):
        for p in peers:
            x_copy(k, p).start()

    half = ni // 2
    side = i // half
    base, far = side * half, (1 - side) * half
    relay, far_relay = half - 1 + side, half - side
    near = [base + lax.rem(i - base + d, half) for d in range(1, half)]

    def share_of(p):
        return pl.ds(pl.multiple_of(p * share, 128), share)

    def lw_copy(p, slot):
        return remote(wv_hbm.at[:, share_of(p)], lw_buf.at[slot], lw_ss.at[p], lw_rs.at[slot], {"island": p})

    def rl_copy(e, slot, where):
        return remote(
            wv_hbm.at[:, share_of(far + e)], rl_buf.at[slot, e], rl_ss.at[e], rl_rs.at[slot, e], {"island": where}
        )

    def pk_copy(e):
        return remote(pk_send.at[e], pk_buf, pk_ss.at[e], pk_rs.at[0], {"island": far + e})

    def pack(e):
        @pl.when(i == relay)
        def _():
            total = wv_v[:, share_of(far + e)].astype(jnp.float32)
            for p in near:
                rl_copy(e, p, p).wait_recv()
                total = total + rl_buf[p, e].astype(jnp.float32)
            level = jnp.max(jnp.max(jnp.abs(total), axis=0, keepdims=True), axis=1, keepdims=True) + 1e-30
            pk_send[e] = to_code(total * (STEPS / level))
            levels_v[6 + e : 7 + e, :] = jnp.broadcast_to(level * (1.0 / STEPS), (1, 128))
            pk_copy(e).start()

    levels_v[...] = jnp.zeros_like(levels_v)

    @pl.when(i != relay)
    def _():
        for e in range(half):
            rl_copy(e, i, relay).start()

    for copy in loads[:3]:
        copy.wait()
    v_buf[f] = attend(q_v, k_v, og_v)

    def v_copy(slot, p, send_sem):
        return remote(v_buf.at[slot], v_buf.at[slot], send_sem, v_rs.at[slot], {"fsdp": p})

    for p in mates:
        v_copy(f, p, v_ss.at[p]).start()
    v_copy(f, sibling, v_ss.at[sibling]).start()
    for p in peers:
        x_copy(EARLY, p).start()
    for p in near:
        lw_copy(p, i).start()

    loads[3].wait()
    widened = x_v[...].astype(jnp.float32)
    average = jnp.mean(widened, axis=1, keepdims=True)
    centered = x_v[...].astype(jnp.float32) - average
    rstd = lax.rsqrt(jnp.mean(centered * centered, axis=1, keepdims=True) + EPSILON)
    square = (tokens, tokens)
    eye = lax.broadcasted_iota(jnp.int32, square, 0) == lax.broadcasted_iota(jnp.int32, square, 1)

    def to_row(column):
        return jnp.sum(jnp.where(eye, jnp.broadcast_to(column, square), 0.0), axis=0, keepdims=True)

    def to_column(row):
        return jnp.sum(jnp.where(eye, jnp.broadcast_to(row, square), 0.0), axis=1, keepdims=True)

    s_buf[f] = jnp.concatenate(
        [to_row(average), to_row(rstd), lang_ref[...].astype(jnp.float32), jnp.zeros((5, tokens), jnp.float32)],
        axis=0,
    )

    def s_copy(slot, p):
        return remote(s_buf.at[slot], s_buf.at[slot], s_ss.at[p], s_rs.at[slot], {"fsdp": p})

    for p in peers:
        s_copy(f, p).start()
    loads[4].wait()
    pack(0)
    for p in mates:
        v_copy(p, p, v_ss.at[p]).wait_recv()
        v_copy(p, sibling, fw_ss.at[p]).start()
    for k in range(EARLY + 1, CHUNKS):
        for p in peers:
            x_copy(k, p).start()
    for e in range(1, half):
        pack(e)

    for copy in own_copies:
        copy.wait()
    for p in peers:
        s_copy(p, p).wait_recv()
    for s in range(nf):
        stats = s_buf[s]
        rows = pl.ds(s * tokens, tokens)
        mean_b[rows, :] = jnp.broadcast_to(to_column(stats[0:1]), square)
        rstd_b[rows, :] = jnp.broadcast_to(to_column(stats[1:2]), square)
        kinds = lax.broadcasted_iota(jnp.int32, (langs, tokens), 0).astype(jnp.float32)
        hot[:, s * tokens : (s + 1) * tokens] = jnp.where(
            jnp.broadcast_to(stats[2:3], (langs, tokens)) == kinds, 1.0, 0.0
        ).astype(jnp.bfloat16)
    v_copy(sibling, sibling, v_ss.at[sibling]).wait_recv()
    for p in others:
        v_copy(p, sibling, v_ss.at[p]).wait_recv()

    def g_copy(k, p, slot):
        rows = pl.ds(pl.multiple_of(k * chunk, 128), chunk)
        return remote(g_send.at[p, rows], g_buf.at[slot, rows], g_ss.at[k, p], g_rs.at[k, slot], {"island": p})

    tile = (8, 128)
    tile_row = lax.broadcasted_iota(jnp.int32, tile, 0)

    def step(k, carry):
        wv_square, gain_square, levels = carry
        for p in peers:
            x_wait(k, p)
        rows = pl.ds(pl.multiple_of(k * chunk, 128), chunk)
        weight = wv_v[rows, :]
        gain = gain_ref[:, pl.ds(pl.multiple_of(f * cols + k * chunk, 128), chunk)]
        values_all = v_buf[...].reshape(nf * tokens, kv_width)
        wide_b[...] = lax.dot_general(values_all, weight, (((1,), (1,)), ((), ())), preferred_element_type=jnp.float32)
        for s in range(nf):
            at = slice(s * tokens, (s + 1) * tokens)
            mean = jnp.concatenate([mean_b[at, :]] * (chunk // tokens), axis=1)
            rstd = jnp.concatenate([rstd_b[at, :]] * (chunk // tokens), axis=1)
            table = hot[:, at]
            standard = (x_buf[k, s].astype(jnp.float32) - mean) * rstd
            gain_rows = lax.dot_general(table, gain, (((0,), (0,)), ((), ())), preferred_element_type=jnp.float32)
            normed[at, :] = (standard * gain_rows).astype(jnp.bfloat16)
            product = standard * (wide_b[at, :] * scale)
            high = product.astype(jnp.bfloat16)
            split_b[0, at, :] = high
            split_b[1, at, :] = (product - high.astype(jnp.float32)).astype(jnp.bfloat16)
        gain_grad = jnp.dot(hot[...], split_b[0], preferred_element_type=jnp.float32) + jnp.dot(
            hot[...], split_b[1], preferred_element_type=jnp.float32
        )
        grad = (
            lax.dot_general(normed[...], values_all, (((0,), (0,)), ((), ())), preferred_element_type=jnp.float32)
            * scale
        )
        level = jnp.max(jnp.max(jnp.abs(grad), axis=0, keepdims=True), axis=1, keepdims=True) + 1e-30
        coded = grad * (STEPS / level)
        for j in range(ni):
            piece = grad[:, j * share : (j + 1) * share]
            g_own[j, rows, :] = piece
            g_send[j, rows, :] = to_code(coded[:, j * share : (j + 1) * share])
            own = slice(j * gain_share, (j + 1) * gain_share)
            gg_send[j, 0:gain_share, rows] = gain[own].astype(jnp.float32)
            gg_send[j, gain_share : 2 * gain_share, rows] = gain_grad[own]
        for p in zpeers:
            g_copy(k, p, i).start()
        return (
            wv_square + jnp.sum(grad * grad, axis=0, keepdims=True),
            gain_square + jnp.sum(gain_grad * gain_grad, axis=0, keepdims=True),
            jnp.where(tile_row == k + 2, jnp.broadcast_to(level, tile), levels),
        )

    start = (
        jnp.zeros((1, kv_width), jnp.float32),
        jnp.zeros((1, chunk), jnp.float32),
        jnp.zeros(tile, jnp.float32),
    )
    wv_square, gain_square, levels = lax.fori_loop(0, CHUNKS, step, start)

    first = tile_row == 0
    sq_buf[f] = jnp.where(
        first,
        jnp.broadcast_to(jnp.sum(wv_square, axis=1, keepdims=True), tile),
        jnp.broadcast_to(jnp.sum(gain_square, axis=1, keepdims=True), tile),
    )

    def sq_copy(slot, p):
        return remote(sq_buf.at[slot], sq_buf.at[slot], sq_ss.at[p], sq_rs.at[slot], {"fsdp": p})

    def gg_copy(p, slot):
        return remote(gg_send.at[p], gg_buf.at[slot], gg_ss.at[p], gg_rs.at[slot], {"island": p})

    for p in peers:
        sq_copy(f, p).start()
    for p in zpeers:
        gg_copy(p, i).start()
    for p in peers:
        sq_copy(p, p).wait_recv()
    norm = jnp.sqrt(jnp.sum(sq_buf[...], axis=0))
    bound = jnp.where(first, CLIP_SHARE * (width * kv_width) ** 0.5, CLIP_SHARE * (langs * width) ** 0.5)
    clip = jnp.minimum(1.0, bound.astype(jnp.float32) / norm)
    coded_clip = clip[0:1] * levels * (1.0 / STEPS)
    clip_buf[i] = jnp.where(tile_row < 2, clip, jnp.where(tile_row < CHUNKS + 2, coded_clip, levels_v[...]))

    def c_copy(slot, p):
        return remote(clip_buf.at[slot], clip_buf.at[slot], c_ss.at[p], c_rs.at[slot], {"island": p})

    for p in zpeers:
        c_copy(i, p).start()
    for p in near:
        lw_copy(p, p).wait_recv()
    for p in zpeers:
        gg_copy(p, p).wait_recv()
        c_copy(p, p).wait_recv()
    remote(pk_send.at[0], pk_buf, pk_ss.at[0], pk_rs.at[0], {"island": far_relay}).wait_recv()

    def wide(row, size):
        return jnp.concatenate([row] * (size // 128), axis=1)

    mine = clip_buf[i]
    own_gain = gg_send[i]
    total = own_gain[0:gain_share] - wide(mine[1:2], cols) * own_gain[gain_share : 2 * gain_share]
    for p in zpeers:
        theirs = gg_buf[p]
        total = total + theirs[0:gain_share] - wide(clip_buf[p][1:2], cols) * theirs[gain_share : 2 * gain_share]
    tot_gain[...] = total
    total = wv_v[:, pl.ds(pl.multiple_of(i * share, 128), share)].astype(jnp.float32) - mine[0:1] * g_own[i]
    for p in near:
        total = total + lw_buf[p].astype(jnp.float32)
    far_levels = clip_buf[far_relay]
    total = total + jnp.where(i == base, far_levels[6:7], far_levels[7:8]) * from_code(pk_buf[...])
    for k in range(CHUNKS):
        rows = slice(k * chunk, (k + 1) * chunk)
        part = total[rows]
        for p in zpeers:
            g_copy(k, p, p).wait_recv()
            part = part - clip_buf[p][k + 2 : k + 3] * from_code(g_buf[p, rows])
        tot_wv[rows, :] = part

    for p in peers:
        for k in range(CHUNKS):
            x_copy(k, p).wait_send()
        s_copy(f, p).wait_send()
        sq_copy(f, p).wait_send()
    for p in mates:
        v_copy(f, p, v_ss.at[p]).wait_send()
        v_copy(p, sibling, fw_ss.at[p]).wait_send()
    v_copy(f, sibling, v_ss.at[sibling]).wait_send()
    for p in near:
        lw_copy(p, i).wait_send()

    @pl.when(i != relay)
    def _():
        for e in range(half):
            rl_copy(e, i, relay).wait_send()

    @pl.when(i == relay)
    def _():
        for e in range(half):
            pk_copy(e).wait_send()

    for p in zpeers:
        gg_copy(p, i).wait_send()
        c_copy(i, p).wait_send()
        for k in range(CHUNKS):
            g_copy(k, p, i).wait_send()


def totals_by_kernel(block_input, lang_ids, queries, saved_keys, out_grad, local_wv, local_gain):
    nf, ni = lax.axis_size("fsdp"), lax.axis_size("island")
    tokens, width = block_input.shape
    kv_width, langs = local_wv.shape[2], local_gain.shape[1]
    cols = width // nf
    chunk, share, gain_share = cols // CHUNKS, kv_width // ni, langs // ni
    bf, f32 = jnp.bfloat16, jnp.float32
    vmem = lambda *shape, dtype=bf: pltpu.VMEM(shape, dtype)
    dma = pltpu.SemaphoreType.DMA
    hbm = pl.BlockSpec(memory_space=pl.ANY)
    held = pl.BlockSpec(memory_space=pltpu.VMEM)
    return pl.pallas_call(
        functools.partial(kernel, nf, ni),
        out_shape=(jax.ShapeDtypeStruct((cols, share), f32), jax.ShapeDtypeStruct((gain_share, cols), f32)),
        in_specs=[hbm, held, hbm, hbm, hbm, hbm, held],
        out_specs=(held, held),
        scratch_shapes=[
            vmem(tokens, width),
            vmem(*queries.shape),
            vmem(*saved_keys.shape),
            vmem(*out_grad.shape),
            vmem(cols, kv_width),
            vmem(CHUNKS, nf, tokens, chunk),
            vmem(nf, tokens, kv_width),
            vmem(nf, 8, tokens, dtype=f32),
            vmem(nf * tokens, tokens, dtype=f32),
            vmem(nf * tokens, tokens, dtype=f32),
            vmem(langs, nf * tokens),
            vmem(nf * tokens, chunk),
            vmem(nf * tokens, chunk, dtype=f32),
            vmem(2, nf * tokens, chunk),
            vmem(ni, cols, share, dtype=f32),
            vmem(ni, cols, share, dtype=jnp.int16),
            vmem(ni, cols, share, dtype=jnp.int16),
            vmem(ni, cols, share),
            vmem(ni, ni // 2, cols, share),
            vmem(ni // 2, cols, share, dtype=jnp.int16),
            vmem(cols, share, dtype=jnp.int16),
            vmem(8, 128, dtype=f32),
            vmem(ni, 2 * gain_share, cols, dtype=f32),
            vmem(ni, 2 * gain_share, cols, dtype=f32),
            vmem(nf, 8, 128, dtype=f32),
            vmem(ni, 8, 128, dtype=f32),
            dma((5,)),
            dma((CHUNKS,)),
            dma((CHUNKS, nf)),
            dma((CHUNKS, nf)),
            dma((ni,)),
            dma((ni,)),
            dma((ni // 2,)),
            dma((ni, ni // 2)),
            dma((ni // 2,)),
            dma((1,)),
            dma((nf,)),
            dma((nf,)),
            dma((nf,)),
            dma((nf,)),
            dma((nf,)),
            dma((CHUNKS, ni)),
            dma((CHUNKS, ni)),
            dma((ni,)),
            dma((ni,)),
            dma((nf,)),
            dma((nf,)),
            dma((ni,)),
            dma((ni,)),
        ],
        compiler_params=pltpu.CompilerParams(
            collective_id=0, has_side_effects=True, vmem_limit_bytes=60 * 1024 * 1024
        ),
    )(block_input, lang_ids[None, :], queries, saved_keys, out_grad, local_wv[0], local_gain[0])


def body(
    block_input,
    lang_ids,
    queries,
    saved_keys,
    out_grad,
    local_wv,
    local_gain,
    outer_wv,
    wv_momentum,
    outer_gain,
    gain_momentum,
):
    island_count = lax.axis_size("island")
    fsdp_count = lax.axis_size("fsdp")
    whole_tiles = (
        local_wv.shape[2] % (128 * island_count) == 0
        and local_gain.shape[1] % (4 * island_count) == 0
        and block_input.shape[1] % (128 * CHUNKS * fsdp_count) == 0
        and block_input.shape[0] == 128
        and fsdp_count % 2 == 0
        and island_count in (2, 4)
    )
    totals = totals_by_kernel if whole_tiles else totals_by_collectives
    total_wv, total_gain = totals(
        block_input, lang_ids, queries, saved_keys, out_grad, local_wv, local_gain
    )
    delta_wv = outer_wv - total_wv / island_count
    momentum_wv = MOMENTUM * wv_momentum + delta_wv
    result_wv = outer_wv - OUTER_RATE * (delta_wv + MOMENTUM * momentum_wv)
    delta_gain = outer_gain - total_gain / island_count
    momentum_gain = MOMENTUM * gain_momentum + delta_gain
    result_gain = outer_gain - OUTER_RATE * (delta_gain + MOMENTUM * momentum_gain)
    return (result_wv, momentum_wv, result_gain, momentum_gain)


def solution(mesh):
    in_specs = (
        P(("island", "fsdp"), None),
        P(("island", "fsdp")),
        P(("island", "fsdp"), None),
        P(("island", "fsdp"), None),
        P(("island", "fsdp"), None),
        P("island", "fsdp", None),
        P("island", None, None),
        P("fsdp", "island"),
        P("fsdp", "island"),
        P("island", "fsdp"),
        P("island", "fsdp"),
    )
    out_specs = (P("fsdp", "island"), P("fsdp", "island"), P("island", "fsdp"), P("island", "fsdp"))
    return jax.shard_map(body, mesh=mesh, in_specs=in_specs, out_specs=out_specs, check_vma=False)
```
